128 devices in a mesh: dom: 16 (over y, z), sub: 8 (over x, core).
Axes of the slice: x: 4, y: 4, z: 4, core: 2. Of those that a mesh axis runs over, the one named last changes fastest.
Arguments:
- fine_latent: bfloat16 [4096, 64, 128], P(('dom', 'sub')), may hold values from -6 to 6
- coarse_latent: bfloat16 [1024, 64, 128], P(('dom', 'sub')), may hold values from -6 to 6
- adj_index: int32 [4096, 16], P(('dom', 'sub')), may hold values from 0 to 79
- adj_weight: bfloat16 [4096, 64, 1024], P(('dom', 'sub')), may hold values from -0.1875 to 0.1875
- interp_slot: int32 [4096, 4], P(('dom', 'sub')), may hold values from 0 to 127
- interp_weight: bfloat16 [4096, 64, 256], P(('dom', 'sub')), may hold values from -0.375 to 0.375
- coarse_send: int32 [128, 128, 1], P(('dom', 'sub')), may hold values from 0 to 7
- halo_sub_send: int32 [128, 8, 4], P(('dom', 'sub')), may hold values from 0 to 31
- halo_dom_send: int32 [128, 2, 8], P(('dom', 'sub')), may hold values from 0 to 31
- block_count: int32 [128], P(('dom', 'sub')), may hold values from 16 to 32, as said below
- w_in: bfloat16 [2, 384, 128], replicated, may hold values from -0.3125 to 0.3125
- b_in: float32 [2, 128], replicated, may hold values from -3 to 3
- w_out: bfloat16 [2, 128, 128], replicated, may hold values from -0.5 to 0.5
- ln_gain: float32 [2, 128], replicated, may hold values from 0.25 to 1.75
Outputs:
- fine_out: bfloat16 [4096, 64, 128], P(('dom', 'sub'))
The draws below stay inside these ranges and needn't reach their ends.
Inputs may be any that keep to these rules, and one draw needn't show every extreme that they name: `block_count`: some device has all 32 blocks live and some has half of them.
All inputs are finite; a program needn't handle non-finite values.
Results may differ from the reference program's by a relative error of at most 0.0058.
Values may be sent and summed in bfloat16 or wider, within the bound.
No kernel may reach another device: no remote copies, remote signals or barrier semaphores. Data moves between devices by JAX's collectives and lax.ppermute only.
A program may use at most 64 MiB of HBM per device.

```python
import jax
import jax.numpy as jnp
from jax import lax

BLK = 64
LAT = 128
FBLK_DEV = 32
CBLK_DEV = 8
K_A = 16
K_I = 4
SLOTS = 1
HS = 4
HD = 8
STEPS = 2
SHARDS = 128
POOL = 80
FINE_BLKS = 4096
COARSE_BLKS = 1024
N_DOM = 16
N_SUB = 8


def draw_block_count(key, part):
    lowest = FBLK_DEV // 2
    counts = jax.random.randint(key, (SHARDS,), lowest, FBLK_DEV + 1)
    order = jax.random.permutation(jax.random.fold_in(key, 7), SHARDS)
    counts = counts.at[order[0]].set(FBLK_DEV).at[order[1]].set(lowest)
    return counts.astype(jnp.int32)


def plant(entries, key, smallest, largest):
    shape = entries.shape
    place = [jax.random.randint(jax.random.fold_in(key, axis), (), 0, shape[axis]) for axis in range(len(shape))]
    entries = entries.at[tuple(place)].set(smallest)
    longest = shape.index(max(shape))
    place[longest] = (place[longest] + 1) % shape[longest]
    return entries.at[tuple(place)].set(largest)


def block_scale(stream_key, shape, cuts, least, high):
    def one(dim, shards_of):
        draws = jax.random.uniform(jax.random.fold_in(jax.random.fold_in(stream_key, 6), dim), (shards_of,), jnp.float32, least / len(cuts), high / len(cuts))
        return jnp.repeat(jnp.exp(draws), shape[dim] // shards_of).reshape((-1,) + (1,) * (len(shape) - dim - 1))

    loudness = one(*cuts[0])
    for cut in cuts[1:]:
        loudness = loudness * one(*cut)
    return loudness


def scatter_about(key, dims, width, bound, pieces=(), kind=jnp.bfloat16):
    drawn = width * jax.random.normal(key, dims, jnp.float32)
    if pieces:
        drawn = drawn * block_scale(key, dims, pieces, -0.22, 0.18)
    return jnp.clip(drawn, -bound, bound).astype(kind)


def setup_inputs(seed: int = 0) -> dict:
    key_of = jax.random.split(jax.random.key(seed), 15)
    fine_latent = scatter_about(key_of[0], (FINE_BLKS, BLK, LAT), 1.0, 6.0, ((0, 128),))
    coarse_latent = scatter_about(key_of[1], (COARSE_BLKS, BLK, LAT), 1.0, 6.0, ((0, 128),))
    adj_index = plant(jax.random.randint(key_of[2], (FINE_BLKS, K_A), 0, POOL), jax.random.fold_in(key_of[2], 1), 0, POOL - 1).astype(jnp.int32)
    adj_weight = scatter_about(key_of[3], (FINE_BLKS, BLK, K_A * BLK), (K_A * BLK) ** -0.5, 0.1875, ((0, 128),))
    interp_slot = plant(jax.random.randint(key_of[4], (FINE_BLKS, K_I), 0, SHARDS * SLOTS), jax.random.fold_in(key_of[4], 1), 0, (SHARDS * SLOTS) - 1).astype(jnp.int32)
    interp_weight = scatter_about(key_of[5], (FINE_BLKS, BLK, K_I * BLK), (K_I * BLK) ** -0.5, 0.375, ((0, 128),))
    coarse_send = plant(jax.random.randint(key_of[6], (SHARDS, SHARDS, SLOTS), 0, CBLK_DEV), jax.random.fold_in(key_of[6], 1), 0, CBLK_DEV - 1).astype(jnp.int32)
    halo_sub_send = plant(jax.random.randint(key_of[7], (SHARDS, N_SUB, HS), 0, FBLK_DEV), jax.random.fold_in(key_of[7], 1), 0, FBLK_DEV - 1).astype(jnp.int32)
    halo_dom_send = plant(jax.random.randint(key_of[8], (SHARDS, 2, HD), 0, FBLK_DEV), jax.random.fold_in(key_of[8], 1), 0, FBLK_DEV - 1).astype(jnp.int32)
    block_count = draw_block_count(jax.random.fold_in(key_of[14], 71), 0)
    w_in = scatter_about(key_of[10], (STEPS, 3 * LAT, LAT), (3 * LAT) ** -0.5, 0.3125)
    b_in = scatter_about(key_of[11], (STEPS, LAT), 0.5, 3.0, (), jnp.float32)
    w_out = scatter_about(key_of[12], (STEPS, LAT, LAT), LAT ** -0.5, 0.5)
    ln_gain = jnp.clip(1.0 + 0.15 * jax.random.normal(key_of[13], (STEPS, LAT), jnp.float32), 0.25, 1.75)
    return dict(fine_latent=fine_latent, coarse_latent=coarse_latent, adj_index=adj_index, adj_weight=adj_weight, interp_slot=interp_slot, interp_weight=interp_weight, coarse_send=coarse_send, halo_sub_send=halo_sub_send, halo_dom_send=halo_dom_send, block_count=block_count, w_in=w_in, b_in=b_in, w_out=w_out, ln_gain=ln_gain)


def layer_norm(values, ln_scale):
    average = lax.optimization_barrier(jnp.mean(values, axis=-1, keepdims=True))
    centred = values - average
    variance = lax.optimization_barrier(jnp.mean(centred * centred, axis=-1, keepdims=True))
    return centred * lax.rsqrt(variance + 1e-05) * ln_scale

def node_update(latent, summed, interp, w_first, b_first, w_second, ln_scale, live_mask):
    joined = jnp.concatenate([latent, summed, interp], axis=-1)
    hidden = jnp.einsum('bic,cl->bil', joined.astype(jnp.float32), w_first.astype(jnp.float32)) + b_first
    hidden = jax.nn.relu(hidden).astype(jnp.bfloat16)
    output = jnp.einsum('bic,cl->bil', hidden.astype(jnp.float32), w_second.astype(jnp.float32))
    updated = latent.astype(jnp.float32) + layer_norm(output, ln_scale)
    return jnp.where(live_mask[:, None, None], updated, jnp.zeros_like(updated)).astype(jnp.bfloat16)

def reference(fine_latent, coarse_latent, adj_index, adj_weight, interp_slot, interp_weight, coarse_send, halo_sub_send, halo_dom_send, block_count, w_in, b_in, w_out, ln_gain):
    fine = fine_latent.reshape(SHARDS, FBLK_DEV, BLK, LAT)
    adj_ids = adj_index.reshape(SHARDS, FBLK_DEV, K_A)
    adj_wts = adj_weight.reshape(SHARDS, FBLK_DEV, BLK, K_A * BLK)
    slot_ids = interp_slot.reshape(SHARDS, FBLK_DEV, K_I)
    interp_wts = interp_weight.reshape(SHARDS, FBLK_DEV, BLK, K_I * BLK)
    sources = jnp.arange(SHARDS, dtype=jnp.int32)
    global_ids = sources[:, None, None] * CBLK_DEV + coarse_send
    slot_table = jnp.transpose(global_ids, (1, 0, 2)).reshape(SHARDS, SHARDS * SLOTS)

    def interp_one(device):
        coarse_ids = slot_table[device][slot_ids[device]]
        coarse_rows = coarse_latent[coarse_ids].reshape(FBLK_DEV, K_I * BLK, LAT)
        mixed = jnp.einsum('bim,bml->bil', interp_wts[device].astype(jnp.float32), coarse_rows.astype(jnp.float32))
        return mixed.astype(jnp.bfloat16)
    interp = lax.map(interp_one, sources)
    live_all = jnp.arange(FBLK_DEV, dtype=jnp.int32)[None, :] < block_count[:, None]
    latent = fine
    for layer_step in range(STEPS):

        def update_one(device, latent=latent, layer_step=layer_step):
            dom_index = device // N_SUB
            sub_index = device % N_SUB
            peer_ids = dom_index * N_SUB + jnp.arange(N_SUB, dtype=jnp.int32)
            sub_blocks = halo_sub_send[peer_ids, sub_index]
            got_sub = latent[peer_ids[:, None], sub_blocks].reshape(N_SUB * HS, BLK, LAT)
            below_id = jnp.maximum(device - N_SUB, 0)
            above_id = jnp.minimum(device + N_SUB, SHARDS - 1)
            from_below = latent[below_id][halo_dom_send[below_id, 0]]
            from_below = jnp.where(dom_index > 0, from_below, jnp.zeros_like(from_below))
            from_above = latent[above_id][halo_dom_send[above_id, 1]]
            from_above = jnp.where(dom_index < N_DOM - 1, from_above, jnp.zeros_like(from_above))
            block_pool = jnp.concatenate([latent[device], got_sub, from_below, from_above], axis=0)
            tile_rows = block_pool[adj_ids[device]].reshape(FBLK_DEV, K_A * BLK, LAT)
            summed = jnp.einsum('bim,bml->bil', adj_wts[device].astype(jnp.float32), tile_rows.astype(jnp.float32)).astype(jnp.bfloat16)
            return node_update(latent[device], summed, interp[device], w_in[layer_step], b_in[layer_step], w_out[layer_step], ln_gain[layer_step], live_all[device])
        latent = lax.map(update_one, sources)
    return latent.reshape(SHARDS * FBLK_DEV, BLK, LAT)
```

```python
import functools

import jax
import jax.numpy as jnp
from jax import lax
from jax.experimental import pallas as pl
from jax.experimental.pallas import tpu as pltpu
from jax.sharding import PartitionSpec as P

BF16 = jnp.bfloat16
F32 = jnp.float32
SMEM = pl.BlockSpec(memory_space=pltpu.SMEM)
ANY = pl.BlockSpec(memory_space=pl.ANY)
GROUP = 4


def whole(*shape):
    return pl.BlockSpec(shape, lambda i: (0,) * len(shape))


def rows_of(*shape):
    return pl.BlockSpec(shape, lambda i: (i,) + (0,) * (len(shape) - 1))


def params(mib):
    return pltpu.CompilerParams(vmem_limit_bytes=mib << 20)


def coarse_pick_kernel(ids, table, out):
    base = pl.program_id(0) * out.shape[0]
    for slot in range(out.shape[0]):
        out[slot] = table[ids[0, base + slot]]


def coarse_pick(coarse, ids):
    slots = ids.shape[1]
    step = slots // 4
    return pl.pallas_call(
        coarse_pick_kernel,
        grid=(4,),
        in_specs=[SMEM, whole(*coarse.shape)],
        out_specs=rows_of(step, *coarse.shape[1:]),
        out_shape=jax.ShapeDtypeStruct((slots,) + coarse.shape[1:], coarse.dtype),
        compiler_params=params(8),
        name="coarse_pick",
    )(ids, coarse)


def copy_halo(latent, sub_ids, dom_ids, sub_out, up_out, down_out):
    per_peer, peers = sub_ids.shape
    for peer in range(peers):
        for slot in range(per_peer):
            sub_out[peer * per_peer + slot] = latent[sub_ids[slot, peer]]
    for slot in range(dom_ids.shape[1]):
        up_out[slot] = latent[dom_ids[0, slot]]
        down_out[slot] = latent[dom_ids[1, slot]]


def halo_pick_kernel(sub_ids, dom_ids, latent, sub_out, up_out, down_out):
    copy_halo(latent, sub_ids, dom_ids, sub_out, up_out, down_out)


def halo_shapes(latent, sub_ids, dom_ids):
    tail = latent.shape[1:]
    return [
        jax.ShapeDtypeStruct((sub_ids.size,) + tail, latent.dtype),
        jax.ShapeDtypeStruct((dom_ids.shape[1],) + tail, latent.dtype),
        jax.ShapeDtypeStruct((dom_ids.shape[1],) + tail, latent.dtype),
    ]


def halo_pick(latent, sub_ids, dom_ids):
    shapes = halo_shapes(latent, sub_ids, dom_ids)
    return pl.pallas_call(
        halo_pick_kernel,
        grid=(1,),
        in_specs=[SMEM, SMEM, whole(*latent.shape)],
        out_specs=[whole(*s.shape) for s in shapes],
        out_shape=shapes,
        compiler_params=params(8),
        name="halo_pick",
    )(sub_ids, dom_ids, latent)


def fill_pool(pool, sems, parts):
    copies = []
    start = 0
    for position, part in enumerate(parts):
        count = part.shape[0]
        copies.append(
            pltpu.make_async_copy(part, pool.at[pl.ds(start, count)], sems.at[position])
        )
        start += count
    for copy in copies:
        copy.start()
    for copy in copies:
        copy.wait()


def tile_product(weight_ref, index, table, ids, block, width):
    total = None
    rows = table.shape[1]
    for first in range(0, ids.shape[0], width):
        gathered = jnp.concatenate(
            [table[ids[first + tile, block]] for tile in range(width)], axis=0
        )
        weights = weight_ref[index, :, first * rows : (first + width) * rows]
        part = jnp.dot(weights, gathered, preferred_element_type=F32)
        total = part if total is None else total + part
    return total


def finish(hidden_sum, latent, w_out, gain, live):
    hidden = jnp.maximum(hidden_sum, 0.0).astype(BF16)
    out = jnp.dot(hidden, w_out, preferred_element_type=F32)
    average = jnp.mean(out, axis=-1, keepdims=True)
    centred = out - average
    variance = jnp.mean(centred * centred, axis=-1, keepdims=True)
    normed = centred * lax.rsqrt(variance + 1e-05) * gain
    updated = latent.astype(F32) + normed
    return jnp.where(live, updated, 0.0).astype(BF16)


def live_rows(count, step, rows):
    first = step * GROUP * rows
    index = first + lax.broadcasted_iota(jnp.int32, (GROUP * rows, 1), 0)
    return index < count * rows


def adjacency_kernel(t, ids, latent, sub, below, above, weights, w_in, b_in, out, pool, sems):
    step = pl.program_id(0)

    @pl.when(step == 0)
    def _():
        fill_pool(pool, sems, (latent, sub, below, above))

    lat = pool.shape[2]
    summed = jnp.concatenate(
        [
            tile_product(weights, g, pool, ids, step * GROUP + g, 4).astype(BF16)
            for g in range(GROUP)
        ],
        axis=0,
    )
    own = pool[pl.ds(step * GROUP, GROUP)].reshape(summed.shape)
    joined = jnp.concatenate([own, summed], axis=1)
    out[...] = jnp.dot(joined, w_in[t, : 2 * lat], preferred_element_type=F32) + b_in[t : t + 1]


def adjacency(t, latent, sub, below, above, ids, weights, w_in, b_in):
    blocks, rows, lat = latent.shape
    pool = latent.shape[0] + sub.shape[0] + below.shape[0] + above.shape[0]
    return pl.pallas_call(
        functools.partial(adjacency_kernel, t),
        grid=(blocks // GROUP,),
        in_specs=[
            SMEM,
            ANY,
            ANY,
            ANY,
            ANY,
            rows_of(GROUP, rows, weights.shape[2]),
            whole(*w_in.shape),
            whole(*b_in.shape),
        ],
        out_specs=rows_of(GROUP * rows, lat),
        out_shape=jax.ShapeDtypeStruct((blocks * rows, lat), F32),
        scratch_shapes=[
            pltpu.VMEM((pool, rows, lat), BF16),
            pltpu.SemaphoreType.DMA((4,)),
        ],
        compiler_params=params(16),
        name="adjacency",
    )(ids, latent, sub, below, above, weights, w_in, b_in)


def first_step_kernel(
    ids, sub_ids, dom_ids, count, received, weights, begun, latent, w_in, w_out, gain,
    h_out, interp_out, sub_out, up_out, down_out,
):
    step = pl.program_id(0)
    rows, lat = latent.shape[1:]
    interp = jnp.concatenate(
        [
            tile_product(weights, g, received, ids, step * GROUP + g, 4).astype(BF16)
            for g in range(GROUP)
        ],
        axis=0,
    )
    interp_out[...] = interp
    total = begun[...] + jnp.dot(interp, w_in[0, 2 * lat :], preferred_element_type=F32)
    new = finish(
        total,
        latent[...].reshape(GROUP * rows, lat),
        w_out[0],
        gain[0:1],
        live_rows(count[0], step, rows),
    )
    h_out[pl.ds(step * GROUP, GROUP)] = new.reshape(GROUP, rows, lat)

    @pl.when(step == pl.num_programs(0) - 1)
    def _():
        copy_halo(h_out, sub_ids, dom_ids, sub_out, up_out, down_out)


def first_step(received, ids, weights, begun, latent, w_in, w_out, gain, count, sub_ids, dom_ids):
    blocks, rows, lat = latent.shape
    halos = halo_shapes(latent, sub_ids, dom_ids)
    return pl.pallas_call(
        first_step_kernel,
        grid=(blocks // GROUP,),
        in_specs=[
            SMEM,
            SMEM,
            SMEM,
            SMEM,
            whole(*received.shape),
            rows_of(GROUP, rows, weights.shape[2]),
            rows_of(GROUP * rows, lat),
            rows_of(GROUP, rows, lat),
            whole(*w_in.shape),
            whole(*w_out.shape),
            whole(*gain.shape),
        ],
        out_specs=[whole(*latent.shape), rows_of(GROUP * rows, lat)]
        + [whole(*s.shape) for s in halos],
        out_shape=[
            jax.ShapeDtypeStruct(latent.shape, BF16),
            jax.ShapeDtypeStruct((blocks * rows, lat), BF16),
        ]
        + halos,
        compiler_params=params(24),
        name="first_step",
    )(ids, sub_ids, dom_ids, count, received, weights, begun, latent, w_in, w_out, gain)


def begin_kernel(t, latent, interp, w_in, b_in, out):
    lat = latent.shape[1]
    own = jnp.dot(latent[...], w_in[t, :lat], preferred_element_type=F32)
    coarse = jnp.dot(interp[...], w_in[t, 2 * lat :], preferred_element_type=F32)
    out[...] = own + coarse + b_in[t : t + 1]


def begin(t, latent, interp, w_in, b_in):
    total, lat = interp.shape
    return pl.pallas_call(
        functools.partial(begin_kernel, t),
        grid=(4,),
        in_specs=[
            rows_of(total // 4, lat),
            rows_of(total // 4, lat),
            whole(*w_in.shape),
            whole(*b_in.shape),
        ],
        out_specs=rows_of(total // 4, lat),
        out_shape=jax.ShapeDtypeStruct((total, lat), F32),
        compiler_params=params(8),
        name="begin",
    )(latent.reshape(total, lat), interp, w_in, b_in)


def last_step_kernel(
    t, ids, count, latent, sub, below, above, weights, begun, w_in, w_out, gain, out, pool, sems
):
    step = pl.program_id(0)

    @pl.when(step == 0)
    def _():
        fill_pool(pool, sems, (latent, sub, below, above))

    rows, lat = pool.shape[1:]
    summed = jnp.concatenate(
        [
            tile_product(weights, g, pool, ids, step * GROUP + g, 4).astype(BF16)
            for g in range(GROUP)
        ],
        axis=0,
    )
    total = begun[...] + jnp.dot(summed, w_in[t, lat : 2 * lat], preferred_element_type=F32)
    own = pool[pl.ds(step * GROUP, GROUP)].reshape(summed.shape)
    new = finish(total, own, w_out[t], gain[t : t + 1], live_rows(count[0], step, rows))
    out[...] = new.reshape(GROUP, rows, lat)


def last_step(t, latent, sub, below, above, ids, weights, begun, w_in, w_out, gain, count):
    blocks, rows, lat = latent.shape
    pool = latent.shape[0] + sub.shape[0] + below.shape[0] + above.shape[0]
    return pl.pallas_call(
        functools.partial(last_step_kernel, t),
        grid=(blocks // GROUP,),
        in_specs=[
            SMEM,
            SMEM,
            ANY,
            ANY,
            ANY,
            ANY,
            rows_of(GROUP, rows, weights.shape[2]),
            rows_of(GROUP * rows, lat),
            whole(*w_in.shape),
            whole(*w_out.shape),
            whole(*gain.shape),
        ],
        out_specs=rows_of(GROUP, rows, lat),
        out_shape=jax.ShapeDtypeStruct(latent.shape, BF16),
        scratch_shapes=[
            pltpu.VMEM((pool, rows, lat), BF16),
            pltpu.SemaphoreType.DMA((4,)),
        ],
        compiler_params=params(16),
        name="last_step",
    )(ids, count, latent, sub, below, above, weights, begun, w_in, w_out, gain)


def exchange(sub, up, down):
    last = lax.axis_size("dom") - 1
    got_sub = lax.all_to_all(sub, "sub", split_axis=0, concat_axis=0, tiled=True)
    below = lax.ppermute(up, "dom", [(i, i + 1) for i in range(last)])
    above = lax.ppermute(down, "dom", [(i + 1, i) for i in range(last)])
    return got_sub, below, above


def per_device(
    fine_latent,
    coarse_latent,
    adj_index,
    adj_weight,
    interp_slot,
    interp_weight,
    coarse_send,
    halo_sub_send,
    halo_dom_send,
    block_count,
    w_in,
    b_in,
    w_out,
    ln_gain,
):
    payload = coarse_pick(coarse_latent, coarse_send.reshape(1, -1))
    received = lax.all_to_all(payload, ("dom", "sub"), split_axis=0, concat_axis=0, tiled=True)
    sub_ids = halo_sub_send[0].T
    dom_ids = halo_dom_send[0]
    adj_ids = adj_index.T
    halo = exchange(*halo_pick(fine_latent, sub_ids, dom_ids))
    begun = adjacency(0, fine_latent, *halo, adj_ids, adj_weight, w_in, b_in)
    latent, interp, *picked = first_step(
        received, interp_slot.T, interp_weight, begun, fine_latent, w_in, w_out, ln_gain,
        block_count, sub_ids, dom_ids,
    )
    halo = exchange(*picked)
    begun = begin(1, latent, interp, w_in, b_in)
    return last_step(
        1, latent, *halo, adj_ids, adj_weight, begun, w_in, w_out, ln_gain, block_count
    )


def solution(mesh):
    split = ("dom", "sub")
    placed = (
        P(split, None, None),
        P(split, None, None),
        P(split, None),
        P(split, None, None),
        P(split, None),
        P(split, None, None),
        P(split, None, None),
        P(split, None, None),
        P(split, None, None),
        P(split),
        P(),
        P(),
        P(),
        P(),
    )
    return jax.shard_map(
        per_device,
        mesh=mesh,
        in_specs=placed,
        out_specs=P(split, None, None),
        check_vma=False,
    )
```

```python
import functools

import jax
import jax.numpy as jnp
from jax import lax
from jax.experimental import pallas as pl
from jax.experimental.pallas import tpu as pltpu
from jax.sharding import PartitionSpec as P

BF16 = jnp.bfloat16
F32 = jnp.float32
SMEM = pl.BlockSpec(memory_space=pltpu.SMEM)
VMEM = pl.BlockSpec(memory_space=pltpu.VMEM)
ANY = pl.BlockSpec(memory_space=pl.ANY)
CHUNKS = 4


def in_hbm(array):
    return pltpu.with_memory_space_constraint(array, pltpu.HBM)


def params(mib):
    return pltpu.CompilerParams(vmem_limit_bytes=mib << 20)


def chunked(source, target, sems, parts=CHUNKS):
    size = source.shape[0] // parts
    return [
        pltpu.make_async_copy(
            source.at[pl.ds(part * size, size)], target.at[pl.ds(part * size, size)], sems.at[part]
        )
        for part in range(parts)
    ]


def start(copies):
    for copy in copies:
        copy.start()


def wait(copies):
    for copy in copies:
        copy.wait()


def coarse_pick_kernel(ids, table, out, staged, sems):
    copies = chunked(staged, out, sems)
    size = staged.shape[0] // len(copies)
    for part, copy in enumerate(copies):
        for slot in range(part * size, (part + 1) * size):
            staged[slot] = table[ids[0, slot]]
        copy.start()
    wait(copies)


def coarse_pick(coarse, ids):
    shape = (ids.shape[1],) + coarse.shape[1:]
    return pl.pallas_call(
        coarse_pick_kernel,
        in_specs=[SMEM, VMEM],
        out_specs=ANY,
        out_shape=pltpu.HBM(shape, BF16),
        scratch_shapes=[pltpu.VMEM(shape, BF16), pltpu.SemaphoreType.DMA((CHUNKS,))],
        compiler_params=params(8),
        name="coarse_pick",
    )(ids, in_hbm(coarse))


def send_halo(latent, sub_ids, dom_ids, staged, outs, sems):
    slots, peers = sub_ids.shape
    per_way = dom_ids.shape[1]
    sizes = [slots * peers, per_way, per_way]
    copies = []
    first = 0
    for out, size, sem in zip(outs, sizes, range(3)):
        copies.append(pltpu.make_async_copy(staged.at[pl.ds(first, size)], out, sems.at[sem]))
        first += size
    for peer in range(peers):
        for slot in range(slots):
            staged[peer * slots + slot] = latent[sub_ids[slot, peer]]
    copies[0].start()
    for way in range(2):
        for slot in range(per_way):
            staged[sizes[0] + way * per_way + slot] = latent[dom_ids[way, slot]]
        copies[1 + way].start()
    return copies


def halo_pick_kernel(sub_ids, dom_ids, latent, after, sub_out, up_out, down_out, staged, sems):
    del after
    wait(send_halo(latent, sub_ids, dom_ids, staged, (sub_out, up_out, down_out), sems))


def halo_shapes(latent, sub_ids, dom_ids):
    tail = latent.shape[1:]
    return [
        pltpu.HBM((count,) + tail, BF16)
        for count in (sub_ids.size, dom_ids.shape[1], dom_ids.shape[1])
    ]


def halo_scratch(latent, sub_ids, dom_ids):
    count = sub_ids.size + dom_ids.size
    return [pltpu.VMEM((count,) + latent.shape[1:], BF16), pltpu.SemaphoreType.DMA((3,))]


def halo_pick(latent, sub_ids, dom_ids, after):
    return pl.pallas_call(
        halo_pick_kernel,
        in_specs=[SMEM, SMEM, VMEM, ANY],
        out_specs=[ANY] * 3,
        out_shape=halo_shapes(latent, sub_ids, dom_ids),
        scratch_shapes=halo_scratch(latent, sub_ids, dom_ids),
        compiler_params=params(8),
        name="halo_pick",
    )(sub_ids, dom_ids, in_hbm(latent), in_hbm(after))


def pool_copies(pool, sems, parts):
    copies = []
    first = 0
    for position, part in enumerate(parts):
        count = part.shape[0]
        copies.append(
            pltpu.make_async_copy(part, pool.at[pl.ds(first, count)], sems.at[position])
        )
        first += count
    return copies


def tile_product(weights, table, ids, block, width):
    total = None
    rows = table.shape[1]
    for first in range(0, ids.shape[0], width):
        gathered = jnp.concatenate(
            [table[ids[first + tile, block]] for tile in range(width)], axis=0
        )
        part = jnp.dot(
            weights[block, :, first * rows : (first + width) * rows],
            gathered,
            preferred_element_type=F32,
        )
        total = part if total is None else total + part
    return total.astype(BF16)


def products(weights, table, ids, copies, out):
    rows = table.shape[1]
    size = weights.shape[0] // len(copies)
    for part, copy in enumerate(copies):
        copy.wait()
        for block in range(part * size, (part + 1) * size):
            out[pl.ds(block * rows, rows)] = tile_product(weights, table, ids, block, 4)


def finish(hidden_sum, latent, w_out, gain, live):
    hidden = jnp.maximum(hidden_sum, 0.0).astype(BF16)
    out = jnp.dot(hidden, w_out, preferred_element_type=F32)
    average = jnp.mean(out, axis=-1, keepdims=True)
    centred = out - average
    variance = jnp.mean(centred * centred, axis=-1, keepdims=True)
    normed = centred * lax.rsqrt(variance + 1e-05) * gain
    updated = latent.astype(F32) + normed
    return jnp.where(live, updated, 0.0).astype(BF16)


def live_rows(count, first, size):
    return first + lax.broadcasted_iota(jnp.int32, (size, 1), 0) < count


def adjacency_kernel(
    ids, latent, sub, below, above, weights, w_in, b_in, out,
    pool, held, summed, staged, pool_sems, in_sems, out_sems,
):
    pools = pool_copies(pool, pool_sems, (latent, sub, below, above))
    start(pools)
    arriving = chunked(weights, held, in_sems)
    start(arriving)
    leaving = chunked(staged, out, out_sems)
    wait(pools)
    products(held, pool, ids, arriving, summed)
    rows, lat = pool.shape[1:]
    size = staged.shape[0] // CHUNKS
    for part, copy in enumerate(leaving):
        here = pl.ds(part * size, size)
        own = pool[pl.ds(part * size // rows, size // rows)].reshape(size, lat)
        joined = jnp.concatenate([own, summed[here]], axis=1)
        staged[here] = jnp.dot(joined, w_in[0, : 2 * lat], preferred_element_type=F32) + b_in[0:1]
        copy.start()
    wait(leaving)


def adjacency(latent, sub, below, above, ids, weights, w_in, b_in):
    blocks, rows, lat = latent.shape
    pool = latent.shape[0] + sub.shape[0] + below.shape[0] + above.shape[0]
    return pl.pallas_call(
        adjacency_kernel,
        in_specs=[SMEM, ANY, ANY, ANY, ANY, ANY, VMEM, VMEM],
        out_specs=ANY,
        out_shape=pltpu.HBM((blocks * rows, lat), F32),
        scratch_shapes=[
            pltpu.VMEM((pool, rows, lat), BF16),
            pltpu.VMEM(weights.shape, BF16),
            pltpu.VMEM((blocks * rows, lat), BF16),
            pltpu.VMEM((blocks * rows, lat), F32),
            pltpu.SemaphoreType.DMA((4,)),
            pltpu.SemaphoreType.DMA((CHUNKS,)),
            pltpu.SemaphoreType.DMA((CHUNKS,)),
        ],
        compiler_params=params(24),
        name="adjacency",
    )(ids, in_hbm(latent), sub, below, above, in_hbm(weights), w_in, b_in)


def first_step_kernel(
    ids, sub_ids, dom_ids, count, received, weights, begun, latent, w_in, w_out, gain,
    h_out, interp_out, sub_out, up_out, down_out,
    held, begun_held, own, interp, new, staged, in_sems, more_sems, out_sems, halo_sems,
):
    arriving = chunked(weights, held, in_sems)
    start(arriving)
    more = [
        pltpu.make_async_copy(begun, begun_held, more_sems.at[0]),
        pltpu.make_async_copy(latent, own, more_sems.at[1]),
    ]
    start(more)
    products(held, received, ids, arriving, interp)
    leaving = [
        pltpu.make_async_copy(interp, interp_out, out_sems.at[0]),
        pltpu.make_async_copy(new, h_out, out_sems.at[1]),
    ]
    wait(more)
    blocks, rows, lat = new.shape
    size = blocks * rows
    total = begun_held[...] + jnp.dot(
        interp[...], w_in[0, 2 * lat :], preferred_element_type=F32
    )
    live = live_rows(count[0] * rows, 0, size)
    updated = finish(total, own[...].reshape(size, lat), w_out[0], gain[0:1], live)
    new[...] = updated.reshape(new.shape)
    halos = send_halo(new, sub_ids, dom_ids, staged, (sub_out, up_out, down_out), halo_sems)
    start(leaving)
    wait(halos + leaving)


def first_step(received, ids, weights, begun, latent, w_in, w_out, gain, count, sub_ids, dom_ids):
    blocks, rows, lat = latent.shape
    return pl.pallas_call(
        first_step_kernel,
        in_specs=[SMEM, SMEM, SMEM, SMEM, VMEM, ANY, ANY, ANY, VMEM, VMEM, VMEM],
        out_specs=[ANY] * 5,
        out_shape=[pltpu.HBM(latent.shape, BF16), pltpu.HBM((blocks * rows, lat), BF16)]
        + halo_shapes(latent, sub_ids, dom_ids),
        scratch_shapes=[
            pltpu.VMEM(weights.shape, BF16),
            pltpu.VMEM((blocks * rows, lat), F32),
            pltpu.VMEM(latent.shape, BF16),
            pltpu.VMEM((blocks * rows, lat), BF16),
            pltpu.VMEM(latent.shape, BF16),
            halo_scratch(latent, sub_ids, dom_ids)[0],
            pltpu.SemaphoreType.DMA((CHUNKS,)),
            pltpu.SemaphoreType.DMA((2,)),
            pltpu.SemaphoreType.DMA((2,)),
            pltpu.SemaphoreType.DMA((3,)),
        ],
        compiler_params=params(24),
        name="first_step",
    )(
        ids, sub_ids, dom_ids, count, received, in_hbm(weights), in_hbm(begun), in_hbm(latent),
        w_in, w_out, gain,
    )


def begin_kernel(latent, interp, w_in, b_in, out, own, coarse, staged, in_sems, more_sems, out_sems):
    lat = own.shape[1]
    owns = chunked(latent, own, in_sems)
    coarses = chunked(interp, coarse, more_sems)
    leaving = chunked(staged, out, out_sems)
    start(owns)
    start(coarses)
    size = own.shape[0] // CHUNKS
    for part, copy in enumerate(leaving):
        here = pl.ds(part * size, size)
        owns[part].wait()
        coarses[part].wait()
        total = jnp.dot(own[here], w_in[1, :lat], preferred_element_type=F32)
        total += jnp.dot(coarse[here], w_in[1, 2 * lat :], preferred_element_type=F32)
        staged[here] = total + b_in[1:2]
        copy.start()
    wait(leaving)


def begin(latent, interp, w_in, b_in):
    shape = interp.shape
    return pl.pallas_call(
        begin_kernel,
        in_specs=[ANY, ANY, VMEM, VMEM],
        out_specs=ANY,
        out_shape=pltpu.HBM(shape, F32),
        scratch_shapes=[
            pltpu.VMEM(shape, BF16),
            pltpu.VMEM(shape, BF16),
            pltpu.VMEM(shape, F32),
        ]
        + [pltpu.SemaphoreType.DMA((CHUNKS,))] * 3,
        compiler_params=params(8),
        name="begin",
    )(in_hbm(latent.reshape(shape)), in_hbm(interp), w_in, b_in)


def last_step_kernel(
    ids, count, latent, sub, below, above, weights, begun, w_in, w_out, gain, out,
    pool, held, begun_held, summed, new, pool_sems, in_sems, begun_sem, out_sem,
):
    pools = pool_copies(pool, pool_sems, (latent, sub, below, above))
    start(pools)
    arriving = chunked(weights, held, in_sems)
    start(arriving)
    more = pltpu.make_async_copy(begun, begun_held, begun_sem)
    more.start()
    wait(pools)
    products(held, pool, ids, arriving, summed)
    more.wait()
    blocks, rows, lat = new.shape
    size = blocks * rows
    total = begun_held[...] + jnp.dot(
        summed[...], w_in[1, lat : 2 * lat], preferred_element_type=F32
    )
    own = pool[pl.ds(0, blocks)].reshape(size, lat)
    live = live_rows(count[0] * rows, 0, size)
    new[...] = finish(total, own, w_out[1], gain[1:2], live).reshape(new.shape)
    leaving = pltpu.make_async_copy(new, out, out_sem)
    leaving.start()
    leaving.wait()


def last_step(latent, sub, below, above, ids, weights, begun, w_in, w_out, gain, count):
    blocks, rows, lat = latent.shape
    pool = latent.shape[0] + sub.shape[0] + below.shape[0] + above.shape[0]
    return pl.pallas_call(
        last_step_kernel,
        in_specs=[SMEM, SMEM, ANY, ANY, ANY, ANY, ANY, ANY, VMEM, VMEM, VMEM],
        out_specs=ANY,
        out_shape=pltpu.HBM(latent.shape, BF16),
        scratch_shapes=[
            pltpu.VMEM((pool, rows, lat), BF16),
            pltpu.VMEM(weights.shape, BF16),
            pltpu.VMEM((blocks * rows, lat), F32),
            pltpu.VMEM((blocks * rows, lat), BF16),
            pltpu.VMEM(latent.shape, BF16),
            pltpu.SemaphoreType.DMA((4,)),
            pltpu.SemaphoreType.DMA((CHUNKS,)),
            pltpu.SemaphoreType.DMA,
            pltpu.SemaphoreType.DMA,
        ],
        compiler_params=params(24),
        name="last_step",
    )(
        ids, count, in_hbm(latent), sub, below, above, in_hbm(weights), in_hbm(begun), w_in, w_out, gain
    )


def exchange(sub, up, down):
    last = lax.axis_size("dom") - 1
    got_sub = lax.all_to_all(sub, "sub", split_axis=0, concat_axis=0, tiled=True)
    below = lax.ppermute(up, "dom", [(i, i + 1) for i in range(last)])
    above = lax.ppermute(down, "dom", [(i + 1, i) for i in range(last)])
    return got_sub, below, above


def per_device(
    fine_latent,
    coarse_latent,
    adj_index,
    adj_weight,
    interp_slot,
    interp_weight,
    coarse_send,
    halo_sub_send,
    halo_dom_send,
    block_count,
    w_in,
    b_in,
    w_out,
    ln_gain,
):
    payload = coarse_pick(coarse_latent, coarse_send.reshape(1, -1))
    received = lax.all_to_all(payload, ("dom", "sub"), split_axis=0, concat_axis=0, tiled=True)
    sub_ids = halo_sub_send[0].T
    dom_ids = halo_dom_send[0]
    adj_ids = adj_index.T
    halo = exchange(*halo_pick(fine_latent, sub_ids, dom_ids, payload))
    begun = adjacency(fine_latent, *halo, adj_ids, adj_weight, w_in, b_in)
    latent, interp, *picked = first_step(
        received, interp_slot.T, interp_weight, begun, fine_latent, w_in, w_out, ln_gain,
        block_count, sub_ids, dom_ids,
    )
    halo = exchange(*picked)
    begun = begin(latent, interp, w_in, b_in)
    return last_step(latent, *halo, adj_ids, adj_weight, begun, w_in, w_out, ln_gain, block_count)


def solution(mesh):
    split = ("dom", "sub")
    placed = (
        P(split, None, None),
        P(split, None, None),
        P(split, None),
        P(split, None, None),
        P(split, None),
        P(split, None, None),
        P(split, None, None),
        P(split, None, None),
        P(split, None, None),
        P(split),
        P(),
        P(),
        P(),
        P(),
    )
    return jax.shard_map(
        per_device,
        mesh=mesh,
        in_specs=placed,
        out_specs=P(split, None, None),
        check_vma=False,
    )
```

```python
import functools

import jax
import jax.numpy as jnp
from jax import lax
from jax.experimental import pallas as pl
from jax.experimental.pallas import tpu as pltpu
from jax.sharding import PartitionSpec as P

BF16 = jnp.bfloat16
F32 = jnp.float32
SMEM = pl.BlockSpec(memory_space=pltpu.SMEM)
VMEM = pl.BlockSpec(memory_space=pltpu.VMEM)
ANY = pl.BlockSpec(memory_space=pl.ANY)
CORES = 2


def in_hbm(array):
    return pltpu.with_memory_space_constraint(array, pltpu.HBM)


def in_vmem(array):
    return pltpu.with_memory_space_constraint(array, pltpu.VMEM)


def params(mib):
    return pltpu.CompilerParams(vmem_limit_bytes=mib << 20)


def blocks_like(count, latent):
    return jax.ShapeDtypeStruct((count,) + latent.shape[1:], BF16)


def chunked(source, target, sems):
    parts = sems.shape[0]
    size = source.shape[0] // parts
    return [
        pltpu.make_async_copy(
            source.at[pl.ds(part * size, size)], target.at[pl.ds(part * size, size)], sems.at[part]
        )
        for part in range(parts)
    ]


def start(copies):
    for copy in copies:
        copy.start()


def wait(copies):
    for copy in copies:
        copy.wait()


def copy_for_other_core(latent, sub_ids, out):
    slots, peers = sub_ids.shape
    me = lax.axis_index("sub")
    for way in range(peers // CORES):
        peer = me ^ (way * CORES + 1)
        for slot in range(slots):
            out[way * slots + slot] = latent[sub_ids[slot, peer]]


def copy_for_dom(latent, dom_ids, way, out):
    for slot in range(dom_ids.shape[1]):
        out[slot] = latent[dom_ids[way, slot]]


def copy_for_x(latent, sub_ids, passed, outs):
    slots = sub_ids.shape[0]
    me = lax.axis_index("sub")
    mine = (me % CORES) * slots
    for way, out in enumerate(outs, 1):
        for slot in range(slots):
            out[mine + slot] = latent[sub_ids[slot, me ^ (way * CORES)]]
            out[slots - mine + slot] = passed[way * slots + slot]


def first_hop_kernel(sub_ids, latent, after, other, sems):
    del after
    slots, peers = sub_ids.shape
    me = lax.axis_index("sub")
    copies = []
    for way in range(peers // CORES):
        peer = me ^ (way * CORES + 1)
        for slot in range(slots):
            place = way * slots + slot
            copies.append(
                pltpu.make_async_copy(
                    latent.at[sub_ids[slot, peer]], other.at[place], sems.at[place]
                )
            )
    start(copies)
    wait(copies)


def first_hop(latent, sub_ids, after):
    count = sub_ids.size // CORES
    return pl.pallas_call(
        first_hop_kernel,
        in_specs=[SMEM, ANY, ANY],
        out_specs=VMEM,
        out_shape=blocks_like(count, latent),
        scratch_shapes=[pltpu.SemaphoreType.DMA((count,))],
        compiler_params=params(8),
        name="first_hop",
    )(*map(in_hbm, (sub_ids, latent, after)))


def x_counts(sub_ids):
    slots, peers = sub_ids.shape
    return [slots * CORES] * (peers // CORES - 1)


def pick_kernel(ids, table, out, staged, sems):
    copies = chunked(staged, out, sems)
    size = staged.shape[0] // len(copies)
    for part, copy in enumerate(copies):
        for slot in range(part * size, (part + 1) * size):
            staged[slot] = table[ids[0, slot]]
        copy.start()
    wait(copies)


def pick(coarse, ids):
    shape = (ids.shape[1],) + coarse.shape[1:]
    return pl.pallas_call(
        pick_kernel,
        in_specs=[SMEM, VMEM],
        out_specs=ANY,
        out_shape=pltpu.HBM(shape, BF16),
        scratch_shapes=[pltpu.VMEM(shape, BF16), pltpu.SemaphoreType.DMA((8,))],
        compiler_params=params(8),
        name="pick",
    )(in_hbm(ids), in_hbm(coarse))


def repack_kernel(sub_ids, dom_ids, latent, passed, *outs):
    *pieces, up, down = outs
    copy_for_x(latent, sub_ids, passed, pieces)
    copy_for_dom(latent, dom_ids, 0, up)
    copy_for_dom(latent, dom_ids, 1, down)


def repack(latent, passed, sub_ids, dom_ids):
    counts = x_counts(sub_ids) + [dom_ids.shape[1]] * 2
    return pl.pallas_call(
        repack_kernel,
        in_specs=[SMEM, SMEM, VMEM, VMEM],
        out_specs=[VMEM] * len(counts),
        out_shape=[blocks_like(count, latent) for count in counts],
        compiler_params=params(8),
        name="repack",
    )(sub_ids, dom_ids, latent, passed)


def second_hop(latent, passed, sub_ids, dom_ids):
    *pieces, up, down = repack(latent, passed, sub_ids, dom_ids)
    pieces = along_x(pieces)
    return passed, pieces, along_dom(up, 1), along_dom(down, -1)


def to_other_core(blocks):
    return lax.ppermute(blocks, "sub", [(i, i ^ 1) for i in range(lax.axis_size("sub"))])


def along_x(pieces):
    size = lax.axis_size("sub")
    return [
        lax.ppermute(piece, "sub", [(i, i ^ (way * CORES)) for i in range(size)])
        for way, piece in enumerate(pieces, 1)
    ]


def along_dom(blocks, distance):
    devices = range(lax.axis_size("dom"))
    route = [(i, i + distance) for i in devices if i + distance in devices]
    return lax.ppermute(blocks, "dom", route)


def pool_copies(pool, sems, latent, sub_ids, passed, below, above, pieces):
    slots, peers = sub_ids.shape
    own = latent.shape[0]
    me = lax.axis_index("sub")
    places = [(latent, 0), (passed.at[pl.ds(0, slots)], own + (me ^ 1) * slots)]
    for way, piece in enumerate(pieces, 1):
        places.append((piece, own + (me // CORES ^ way) * CORES * slots))
    end = own + peers * slots
    places += [(below, end), (above, end + below.shape[0])]
    return [
        pltpu.make_async_copy(part, pool.at[pl.ds(first, part.shape[0])], sems.at[position])
        for position, (part, first) in enumerate(places)
    ]


def copy_to_self(pool, sub_ids, own):
    slots = sub_ids.shape[0]
    me = lax.axis_index("sub")
    for slot in range(slots):
        pool[own + me * slots + slot] = pool[sub_ids[slot, me]]


def tile_product(weights, table, ids, block, width):
    total = None
    rows = table.shape[1]
    for first in range(0, ids.shape[0], width):
        gathered = jnp.concatenate(
            [table[ids[first + tile, block]] for tile in range(width)], axis=0
        )
        part = jnp.dot(
            weights[block, :, first * rows : (first + width) * rows],
            gathered,
            preferred_element_type=F32,
        )
        total = part if total is None else total + part
    return total.astype(BF16)


def products(weights, table, ids, out, first, last):
    rows = table.shape[1]
    for block in range(first, last):
        out[pl.ds(block * rows, rows)] = tile_product(weights, table, ids, block, 4)


def node_network(latent, summed, interp, w_in, b_in, w_out, gain, live):
    joined = jnp.concatenate([latent, summed, interp], axis=1)
    hidden = jnp.dot(joined, w_in, preferred_element_type=F32) + b_in
    hidden = jnp.maximum(hidden, 0.0).astype(BF16)
    out = jnp.dot(hidden, w_out, preferred_element_type=F32)
    average = jnp.mean(out, axis=-1, keepdims=True)
    centred = out - average
    variance = jnp.mean(centred * centred, axis=-1, keepdims=True)
    normed = centred * lax.rsqrt(variance + 1e-05) * gain
    updated = latent.astype(F32) + normed
    return jnp.where(live, updated, 0.0).astype(BF16)


def step_blocks(t, pool, summed, interp, w_in, b_in, w_out, gain, count, first, last):
    rows, lat = pool.shape[1:]
    size = (last - first) * rows
    here = pl.ds(first * rows, size)
    index = first * rows + lax.broadcasted_iota(jnp.int32, (size, 1), 0)
    new = node_network(
        pool[pl.ds(first, last - first)].reshape(size, lat),
        summed[here],
        interp[here],
        w_in[t],
        b_in[t : t + 1],
        w_out[t],
        gain[t : t + 1],
        index < count * rows,
    )
    return new.reshape(last - first, rows, lat)


def first_kernel(
    ids, sub_ids, count, slots, received, weights, interp_weights, w_in, b_in, w_out, gain,
    latent, passed, *rest,
):
    ways = sub_ids.shape[1] // CORES - 1
    pieces, (below, above, *rest) = rest[:ways], rest[ways:]
    new, other, interp, held, pool, summed, coarse, slots_held, *net = rest
    net, sems = net[:4], net[4:]
    slot_sem, interp_sems, pool_sems, in_sems, network_sems = sems
    bring = pltpu.make_async_copy(slots, slots_held, slot_sem)
    bring.start()
    coarse_arriving = chunked(interp_weights, coarse, interp_sems)
    start(coarse_arriving)
    pools = pool_copies(pool, pool_sems, latent, sub_ids, passed, below, above, pieces)
    start(pools)
    network = [
        pltpu.make_async_copy(source, target, network_sems.at[position])
        for position, (source, target) in enumerate(zip((w_in, b_in, w_out, gain), net))
    ]
    start(network)
    arriving = chunked(weights, held, in_sems)
    start(arriving)
    bring.wait()
    blocks = held.shape[0]
    size = blocks // len(coarse_arriving)
    for part, copy in enumerate(coarse_arriving):
        copy.wait()
        products(coarse, received, slots_held, interp, part * size, (part + 1) * size)
    wait(pools)
    copy_to_self(pool, sub_ids, blocks)
    size = blocks // len(arriving)
    for part, copy in enumerate(arriving):
        copy.wait()
        products(held, pool, ids, summed, part * size, (part + 1) * size)
    wait(network)
    new[...] = step_blocks(0, pool, summed, interp, *net, count[0], 0, blocks)
    copy_for_other_core(new, sub_ids, other)


def first_step(
    received, slots, interp_weights, latent, halo, ids, weights, w_in, b_in, w_out, gain, count,
    sub_ids, dom_ids,
):
    blocks, rows, lat = latent.shape
    pool = blocks + sub_ids.size + dom_ids.size
    return pl.pallas_call(
        first_kernel,
        in_specs=[SMEM] * 3 + [ANY, VMEM] + [ANY] * (7 + len(halo)),
        out_specs=[VMEM] * 4,
        out_shape=[
            blocks_like(blocks, latent),
            blocks_like(sub_ids.size // CORES, latent),
            jax.ShapeDtypeStruct((blocks * rows, lat), BF16),
            pltpu.VMEM(weights.shape, BF16),
        ],
        scratch_shapes=[
            pltpu.VMEM((pool, rows, lat), BF16),
            pltpu.VMEM((blocks * rows, lat), BF16),
            pltpu.VMEM(interp_weights.shape, BF16),
            pltpu.SMEM(slots.shape, jnp.int32),
            *(pltpu.VMEM(part.shape, part.dtype) for part in (w_in, b_in, w_out, gain)),
            pltpu.SemaphoreType.DMA,
            pltpu.SemaphoreType.DMA((2,)),
            pltpu.SemaphoreType.DMA((1 + len(halo),)),
            pltpu.SemaphoreType.DMA((4,)),
            pltpu.SemaphoreType.DMA((4,)),
        ],
        compiler_params=params(16),
        name="first_step",
    )(
        ids, sub_ids, count, in_hbm(slots), received,
        *map(in_hbm, (weights, interp_weights, w_in, b_in, w_out, gain, latent)), *halo,
    )


def second_kernel(
    ids, sub_ids, count, weights, interp, w_in, b_in, w_out, gain, latent, passed, *rest,
):
    ways = sub_ids.shape[1] // CORES - 1
    pieces, (below, above, *rest) = rest[:ways], rest[ways:]
    out, pool, summed, staged, *net, pool_sems, network_sems, out_sems = rest
    pools = pool_copies(pool, pool_sems, latent, sub_ids, passed, below, above, pieces)
    start(pools)
    network = [
        pltpu.make_async_copy(source, target, network_sems.at[position])
        for position, (source, target) in enumerate(zip((w_in, b_in, w_out, gain), net))
    ]
    start(network)
    wait(pools)
    blocks = latent.shape[0]
    copy_to_self(pool, sub_ids, blocks)
    products(weights, pool, ids, summed, 0, blocks)
    wait(network)
    copies = chunked(staged, out, out_sems)
    size = blocks // len(copies)
    for part, copy in enumerate(copies):
        first, end = part * size, (part + 1) * size
        staged[pl.ds(first, size)] = step_blocks(
            1, pool, summed, interp, *net, count[0], first, end
        )
        copy.start()
    wait(copies)


def second_step(
    latent, halo, weights, interp, ids, w_in, b_in, w_out, gain, count, sub_ids, dom_ids
):
    blocks, rows, lat = latent.shape
    pool = blocks + sub_ids.size + dom_ids.size
    return pl.pallas_call(
        second_kernel,
        in_specs=[SMEM] * 3 + [VMEM, VMEM] + [ANY] * (5 + len(halo)),
        out_specs=ANY,
        out_shape=pltpu.HBM(latent.shape, BF16),
        scratch_shapes=[
            pltpu.VMEM((pool, rows, lat), BF16),
            pltpu.VMEM((blocks * rows, lat), BF16),
            pltpu.VMEM(latent.shape, BF16),
            *(pltpu.VMEM(part.shape, part.dtype) for part in (w_in, b_in, w_out, gain)),
            pltpu.SemaphoreType.DMA((1 + len(halo),)),
            pltpu.SemaphoreType.DMA((4,)),
            pltpu.SemaphoreType.DMA((2,)),
        ],
        compiler_params=params(16),
        name="second_step",
    )(
        ids, sub_ids, count, in_vmem(weights), interp, *map(in_hbm, (w_in, b_in, w_out, gain)),
        latent, *halo,
    )


def per_device(
    fine_latent,
    coarse_latent,
    adj_index,
    adj_weight,
    interp_slot,
    interp_weight,
    coarse_send,
    halo_sub_send,
    halo_dom_send,
    block_count,
    w_in,
    b_in,
    w_out,
    ln_gain,
):
    sub_ids = halo_sub_send[0].T
    dom_ids = halo_dom_send[0]
    adj_ids = adj_index.T
    payload = pick(coarse_latent, coarse_send.reshape(1, -1))
    received = lax.all_to_all(payload, ("dom", "sub"), split_axis=0, concat_axis=0, tiled=True)
    passed = to_other_core(first_hop(fine_latent, sub_ids, payload))
    passed, pieces, below, above = second_hop(fine_latent, passed, sub_ids, dom_ids)
    halo = [passed, *pieces, below, above]
    latent, other, interp, weights = first_step(
        received, interp_slot.T, interp_weight, fine_latent, halo, adj_ids, adj_weight, w_in, b_in,
        w_out, ln_gain, block_count, sub_ids, dom_ids,
    )
    passed = to_other_core(other)
    passed, pieces, below, above = second_hop(latent, passed, sub_ids, dom_ids)
    halo = [passed, *pieces, below, above]
    return second_step(
        latent, halo, weights, interp, adj_ids, w_in, b_in, w_out, ln_gain, block_count, sub_ids,
        dom_ids,
    )


def solution(mesh):
    split = ("dom", "sub")
    placed = (
        P(split, None, None),
        P(split, None, None),
        P(split, None),
        P(split, None, None),
        P(split, None),
        P(split, None, None),
        P(split, None, None),
        P(split, None, None),
        P(split, None, None),
        P(split),
        P(),
        P(),
        P(),
        P(),
    )
    return jax.shard_map(
        per_device,
        mesh=mesh,
        in_specs=placed,
        out_specs=P(split, None, None),
        check_vma=False,
    )
```

```python
import functools

import jax
import jax.numpy as jnp
from jax import lax
from jax.experimental import pallas as pl
from jax.experimental.pallas import tpu as pltpu
from jax.sharding import PartitionSpec as P

BF16 = jnp.bfloat16
F32 = jnp.float32
SMEM = pl.BlockSpec(memory_space=pltpu.SMEM)
VMEM = pl.BlockSpec(memory_space=pltpu.VMEM)
ANY = pl.BlockSpec(memory_space=pl.ANY)
CORES = 2
AHEAD = 2


def in_hbm(array):
    return pltpu.with_memory_space_constraint(array, pltpu.HBM)


def in_vmem(array):
    return pltpu.with_memory_space_constraint(array, pltpu.VMEM)


def params(mib):
    return pltpu.CompilerParams(vmem_limit_bytes=mib << 20)


def blocks_like(count, latent):
    return jax.ShapeDtypeStruct((count,) + latent.shape[1:], BF16)


def chunked(source, target, sems):
    parts = sems.shape[0]
    size = source.shape[0] // parts
    return [
        pltpu.make_async_copy(
            source.at[pl.ds(part * size, size)], target.at[pl.ds(part * size, size)], sems.at[part]
        )
        for part in range(parts)
    ]


def start(copies):
    for copy in copies:
        copy.start()


def wait(copies):
    for copy in copies:
        copy.wait()


def copy_for_other_core(latent, sub_ids, out):
    slots, peers = sub_ids.shape
    me = lax.axis_index("sub")
    for way in range(peers // CORES):
        peer = me ^ (way * CORES + 1)
        for slot in range(slots):
            out[way * slots + slot] = latent[sub_ids[slot, peer]]


def copy_for_dom(latent, dom_ids, way, out):
    for slot in range(dom_ids.shape[1]):
        out[slot] = latent[dom_ids[way, slot]]


def copy_for_x(latent, sub_ids, passed, outs):
    slots = sub_ids.shape[0]
    me = lax.axis_index("sub")
    mine = (me % CORES) * slots
    for way, out in enumerate(outs, 1):
        for slot in range(slots):
            out[mine + slot] = latent[sub_ids[slot, me ^ (way * CORES)]]
            out[slots - mine + slot] = passed[way * slots + slot]


def first_hop_kernel(sub_ids, latent, after, other, sems):
    del after
    slots, peers = sub_ids.shape
    me = lax.axis_index("sub")
    copies = []
    for way in range(peers // CORES):
        peer = me ^ (way * CORES + 1)
        for slot in range(slots):
            place = way * slots + slot
            copies.append(
                pltpu.make_async_copy(
                    latent.at[sub_ids[slot, peer]], other.at[place], sems.at[place]
                )
            )
    start(copies)
    wait(copies)


def first_hop(latent, sub_ids, after):
    count = sub_ids.size // CORES
    return pl.pallas_call(
        first_hop_kernel,
        in_specs=[SMEM, ANY, ANY],
        out_specs=VMEM,
        out_shape=blocks_like(count, latent),
        scratch_shapes=[pltpu.SemaphoreType.DMA((count,))],
        compiler_params=params(8),
        name="first_hop",
    )(*map(in_hbm, (sub_ids, latent, after)))


def x_counts(sub_ids):
    slots, peers = sub_ids.shape
    return [slots * CORES] * (peers // CORES - 1)


def pick_kernel(ids, table, out, ids_held, held, staged, load_sems, sems):
    loads = [
        pltpu.make_async_copy(ids, ids_held, load_sems.at[0]),
        pltpu.make_async_copy(table, held, load_sems.at[1]),
    ]
    start(loads)
    wait(loads)
    copies = chunked(staged, out, sems)
    size = staged.shape[0] // len(copies)
    for part, copy in enumerate(copies):
        for slot in range(part * size, (part + 1) * size):
            staged[slot] = held[ids_held[0, slot]]
        copy.start()
    wait(copies)


def pick(coarse, ids):
    shape = (ids.shape[1],) + coarse.shape[1:]
    return pl.pallas_call(
        pick_kernel,
        in_specs=[ANY, ANY],
        out_specs=ANY,
        out_shape=pltpu.HBM(shape, BF16),
        scratch_shapes=[
            pltpu.SMEM(ids.shape, jnp.int32),
            pltpu.VMEM(coarse.shape, BF16),
            pltpu.VMEM(shape, BF16),
            pltpu.SemaphoreType.DMA((2,)),
            pltpu.SemaphoreType.DMA((8,)),
        ],
        compiler_params=params(8),
        name="pick",
    )(in_hbm(ids), in_hbm(coarse))


def repack_kernel(sub_ids, dom_ids, latent, passed, *outs):
    *pieces, up, down = outs
    copy_for_x(latent, sub_ids, passed, pieces)
    copy_for_dom(latent, dom_ids, 0, up)
    copy_for_dom(latent, dom_ids, 1, down)


def repack(latent, passed, sub_ids, dom_ids):
    counts = x_counts(sub_ids) + [dom_ids.shape[1]] * 2
    return pl.pallas_call(
        repack_kernel,
        in_specs=[SMEM, SMEM, VMEM, VMEM],
        out_specs=[VMEM] * len(counts),
        out_shape=[blocks_like(count, latent) for count in counts],
        compiler_params=params(8),
        name="repack",
    )(sub_ids, dom_ids, latent, passed)


def to_other_core(blocks):
    return lax.ppermute(blocks, "sub", [(i, i ^ 1) for i in range(lax.axis_size("sub"))])


def along_x(pieces):
    size = lax.axis_size("sub")
    return [
        lax.ppermute(piece, "sub", [(i, i ^ (way * CORES)) for i in range(size)])
        for way, piece in enumerate(pieces, 1)
    ]


def along_dom(blocks, distance):
    size = lax.axis_size("dom")
    return lax.ppermute(blocks, "dom", [(i, (i + distance) % size) for i in range(size)])


def second_hop(latent, other, sub_ids, dom_ids):
    passed = to_other_core(other)
    *pieces, up, down = repack(latent, passed, sub_ids, dom_ids)
    return [passed, *along_x(pieces), along_dom(up, 1), along_dom(down, -1)]


def fill_pool(pool, own, sub_ids, passed, pieces, below, above):
    slots, peers = sub_ids.shape
    me = lax.axis_index("sub")
    pool[pl.ds(own + (me ^ 1) * slots, slots)] = passed[:slots]
    for way, piece in enumerate(pieces, 1):
        first = own + (me // CORES ^ way) * CORES * slots
        pool[pl.ds(first, piece.shape[0])] = piece[...]
    end = own + peers * slots
    pool[pl.ds(end, below.shape[0])] = below[...]
    pool[pl.ds(end + below.shape[0], above.shape[0])] = above[...]
    clear_ends(pool, below.shape[0])


def copy_to_self(pool, sub_ids, own):
    slots = sub_ids.shape[0]
    me = lax.axis_index("sub")
    for slot in range(slots):
        pool[own + me * slots + slot] = pool[sub_ids[slot, me]]


def clear_ends(pool, count):
    end = pool.shape[0]
    zeros = jnp.zeros((count,) + pool.shape[1:], pool.dtype)

    @pl.when(lax.axis_index("dom") == 0)
    def _():
        pool[pl.ds(end - 2 * count, count)] = zeros

    @pl.when(lax.axis_index("dom") == lax.axis_size("dom") - 1)
    def _():
        pool[pl.ds(end - count, count)] = zeros


def tile_product(weights, table, ids, block, width):
    total = None
    rows = table.shape[1]
    for first in range(0, ids.shape[0], width):
        gathered = jnp.concatenate(
            [table[ids[first + tile, block]] for tile in range(width)], axis=0
        )
        part = jnp.dot(
            weights[block, :, first * rows : (first + width) * rows],
            gathered,
            preferred_element_type=F32,
        )
        total = part if total is None else total + part
    return total.astype(BF16)


def products(weights, table, ids, out, first, last):
    rows = table.shape[1]
    for block in range(first, last):
        out[pl.ds(block * rows, rows)] = tile_product(weights, table, ids, block, 4)


def node_network(hidden, latent, w_out, gain, live):
    hidden = jnp.maximum(hidden, 0.0).astype(BF16)
    out = jnp.dot(hidden, w_out, preferred_element_type=F32)
    average = jnp.mean(out, axis=-1, keepdims=True)
    centred = out - average
    variance = jnp.mean(centred * centred, axis=-1, keepdims=True)
    normed = centred * lax.rsqrt(variance + 1e-05) * gain
    updated = latent.astype(F32) + normed
    return jnp.where(live, updated, 0.0).astype(BF16)


def live_rows(count, first, size):
    return first + lax.broadcasted_iota(jnp.int32, (size, 1), 0) < count


def first_kernel(
    count, ids, sub_ids, slots, received, weights, interp_weights, w_in, b_in, w_out, gain, latent,
    passed, *rest,
):
    ways = sub_ids.shape[1] // CORES - 1
    pieces, (below, above, *rest) = rest[:ways], rest[ways:]
    pool, other, interp, held, summed, coarse, *rest = rest
    tables, net, sems = rest[:3], rest[3:7], rest[7:]
    table_sems, interp_sems, own_sem, in_sems, network_sems = sems
    tabling = [
        pltpu.make_async_copy(source, target, table_sems.at[position])
        for position, (source, target) in enumerate(zip((slots, sub_ids, ids), tables))
    ]
    start(tabling)
    slots, sub_ids, ids = tables
    coarse_arriving = chunked(interp_weights, coarse, interp_sems)
    arriving = chunked(weights, held, in_sems)
    blocks, rows, lat = latent.shape
    bring = pltpu.make_async_copy(latent, pool.at[pl.ds(0, blocks)], own_sem)
    network = [
        pltpu.make_async_copy(source, target, network_sems.at[position])
        for position, (source, target) in enumerate(zip((w_in, b_in, w_out, gain), net))
    ]
    start(coarse_arriving)
    bring.start()
    queue = arriving + network
    start(queue[:AHEAD])
    queue = queue[AHEAD:]
    w_in, b_in, w_out, gain = net
    wait(tabling)
    fill_pool(pool, blocks, sub_ids, passed, pieces, below, above)
    size = blocks // len(coarse_arriving)
    for part, copy in enumerate(coarse_arriving):
        copy.wait()
        start(queue[:1])
        queue = queue[1:]
        products(coarse, received, slots, interp, part * size, (part + 1) * size)
    bring.wait()
    copy_to_self(pool, sub_ids, blocks)
    size = blocks // len(arriving)
    for part, copy in enumerate(arriving):
        copy.wait()
        start(queue[:2])
        queue = queue[2:]
        products(held, pool, ids, summed, part * size, (part + 1) * size)
    start(queue)
    wait(network)
    own = pool[pl.ds(0, blocks)].reshape(blocks * rows, lat)
    joined = jnp.concatenate([own, summed[...], interp[...]], axis=1)
    hidden = jnp.dot(joined, w_in[0], preferred_element_type=F32) + b_in[0:1]
    live = live_rows(count[0] * rows, 0, blocks * rows)
    new = node_network(hidden, own, w_out[0], gain[0:1], live)
    pool[pl.ds(0, blocks)] = new.reshape(blocks, rows, lat)
    copy_for_other_core(pool, sub_ids, other)
    copy_to_self(pool, sub_ids, blocks)


def first_step(
    received, slots, interp_weights, latent, halo, ids, weights, w_in, b_in, w_out, gain, count,
    sub_ids,
):
    blocks, rows, lat = latent.shape
    pool = blocks + sub_ids.size + 2 * halo[-1].shape[0]
    network = (w_in, b_in, w_out, gain)
    return pl.pallas_call(
        first_kernel,
        in_specs=[SMEM, ANY, ANY, ANY, VMEM] + [ANY] * 7 + [VMEM] * len(halo),
        out_specs=[VMEM] * 4,
        out_shape=[
            pltpu.VMEM((pool, rows, lat), BF16),
            blocks_like(sub_ids.size // CORES, latent),
            jax.ShapeDtypeStruct((blocks * rows, lat), BF16),
            pltpu.VMEM(weights.shape, BF16),
        ],
        scratch_shapes=[
            pltpu.VMEM((blocks * rows, lat), BF16),
            pltpu.VMEM(interp_weights.shape, BF16),
            *(pltpu.SMEM(part.shape, jnp.int32) for part in (slots, sub_ids, ids)),
            *(pltpu.VMEM(part.shape, part.dtype) for part in network),
            pltpu.SemaphoreType.DMA((3,)),
            pltpu.SemaphoreType.DMA((2,)),
            pltpu.SemaphoreType.DMA,
            pltpu.SemaphoreType.DMA((4,)),
            pltpu.SemaphoreType.DMA((4,)),
        ],
        compiler_params=params(16),
        name="first_step",
    )(
        count, *map(in_hbm, (ids, sub_ids, slots)), received,
        *map(in_hbm, (weights, interp_weights, *network, latent)), *halo,
    )


def second_kernel(
    ids, count, weights, interp, w_in, b_in, w_out, gain, pool_in, sub_shape, passed, *rest
):
    del pool_in
    ways = sub_shape.shape[1] // CORES - 1
    pieces, (below, above, *rest) = rest[:ways], rest[ways:]
    pool, out, summed, staged, out_sems = rest
    blocks, rows, lat = staged.shape
    fill_pool(pool, blocks, sub_shape, passed, pieces, below, above)
    products(weights, pool, ids, summed, 0, blocks)
    copies = chunked(staged, out, out_sems)
    size = blocks // len(copies)
    for part, copy in enumerate(copies):
        mine = pl.ds(part * size, size)
        here = pl.ds(part * size * rows, size * rows)
        own = pool[mine].reshape(size * rows, lat)
        joined = jnp.concatenate([own, summed[here], interp[here]], axis=1)
        hidden = jnp.dot(joined, w_in[1], preferred_element_type=F32) + b_in[1:2]
        live = live_rows(count[0] * rows, part * size * rows, size * rows)
        new = node_network(hidden, own, w_out[1], gain[1:2], live)
        staged[mine] = new.reshape(size, rows, lat)
        copy.start()
    wait(copies)


def second_step(pool, halo, weights, interp, ids, w_in, b_in, w_out, gain, count, sub_ids):
    rows, lat = pool.shape[1:]
    blocks = weights.shape[0]
    operands = [ids, count, in_vmem(weights), interp, w_in, b_in, w_out, gain, in_vmem(pool)]
    return pl.pallas_call(
        second_kernel,
        in_specs=[SMEM] * 2 + [VMEM] * 7 + [ANY] + [VMEM] * len(halo),
        out_specs=[VMEM, ANY],
        out_shape=[pltpu.VMEM(pool.shape, BF16), pltpu.HBM((blocks, rows, lat), BF16)],
        input_output_aliases={len(operands) - 1: 0},
        scratch_shapes=[
            pltpu.VMEM((blocks * rows, lat), BF16),
            pltpu.VMEM((blocks, rows, lat), BF16),
            pltpu.SemaphoreType.DMA((2,)),
        ],
        compiler_params=params(16),
        name="second_step",
    )(*operands, sub_ids, *halo)[1]


def per_device(
    fine_latent,
    coarse_latent,
    adj_index,
    adj_weight,
    interp_slot,
    interp_weight,
    coarse_send,
    halo_sub_send,
    halo_dom_send,
    block_count,
    w_in,
    b_in,
    w_out,
    ln_gain,
):
    sub_ids = halo_sub_send[0].T
    dom_ids = halo_dom_send[0]
    adj_ids = adj_index.T
    payload = pick(coarse_latent, coarse_send.reshape(1, -1))
    received = lax.all_to_all(payload, ("dom", "sub"), split_axis=0, concat_axis=0, tiled=True)
    halo = second_hop(fine_latent, first_hop(fine_latent, sub_ids, payload), sub_ids, dom_ids)
    pool, other, interp, weights = first_step(
        received, interp_slot.T, interp_weight, fine_latent, halo, adj_ids, adj_weight, w_in, b_in,
        w_out, ln_gain, block_count, sub_ids,
    )
    halo = second_hop(pool, other, sub_ids, dom_ids)
    return second_step(
        pool, halo, weights, interp, adj_ids, w_in, b_in, w_out, ln_gain, block_count, sub_ids
    )


def solution(mesh):
    split = ("dom", "sub")
    placed = (
        P(split, None, None),
        P(split, None, None),
        P(split, None),
        P(split, None, None),
        P(split, None),
        P(split, None, None),
        P(split, None, None),
        P(split, None, None),
        P(split, None, None),
        P(split),
        P(),
        P(),
        P(),
        P(),
    )
    return jax.shard_map(
        per_device,
        mesh=mesh,
        in_specs=placed,
        out_specs=P(split, None, None),
        check_vma=False,
    )
```

```python
import functools

import jax
import jax.numpy as jnp
from jax import lax
from jax.experimental import pallas as pl
from jax.experimental.pallas import tpu as pltpu
from jax.sharding import PartitionSpec as P

BF16 = jnp.bfloat16
F32 = jnp.float32
SMEM = pl.BlockSpec(memory_space=pltpu.SMEM)
VMEM = pl.BlockSpec(memory_space=pltpu.VMEM)
ANY = pl.BlockSpec(memory_space=pl.ANY)
CORES = 2


def in_hbm(array):
    return pltpu.with_memory_space_constraint(array, pltpu.HBM)


def in_vmem(array):
    return pltpu.with_memory_space_constraint(array, pltpu.VMEM)


def params(mib):
    return pltpu.CompilerParams(vmem_limit_bytes=mib << 20)


def blocks_like(count, latent):
    return jax.ShapeDtypeStruct((count,) + latent.shape[1:], BF16)


def chunked(source, target, sems):
    parts = sems.shape[0]
    size = source.shape[0] // parts
    return [
        pltpu.make_async_copy(
            source.at[pl.ds(part * size, size)], target.at[pl.ds(part * size, size)], sems.at[part]
        )
        for part in range(parts)
    ]


def start(copies):
    for copy in copies:
        copy.start()


def wait(copies):
    for copy in copies:
        copy.wait()


def copy_for_other_core(latent, sub_ids, out):
    slots, peers = sub_ids.shape
    me = lax.axis_index("sub")
    for way in range(peers // CORES):
        peer = me ^ (way * CORES + 1)
        for slot in range(slots):
            out[way * slots + slot] = latent[sub_ids[slot, peer]]


def copy_for_dom(latent, dom_ids, way, out):
    for slot in range(dom_ids.shape[1]):
        out[slot] = latent[dom_ids[way, slot]]


def copy_for_x(latent, sub_ids, passed, outs):
    slots = sub_ids.shape[0]
    me = lax.axis_index("sub")
    mine = (me % CORES) * slots
    for way, out in enumerate(outs, 1):
        for slot in range(slots):
            out[mine + slot] = latent[sub_ids[slot, me ^ (way * CORES)]]
            out[slots - mine + slot] = passed[way * slots + slot]


def first_hop_kernel(sub_ids, latent, after, other, sems):
    del after
    slots, peers = sub_ids.shape
    me = lax.axis_index("sub")
    copies = []
    for way in range(peers // CORES):
        peer = me ^ (way * CORES + 1)
        for slot in range(slots):
            place = way * slots + slot
            copies.append(
                pltpu.make_async_copy(
                    latent.at[sub_ids[slot, peer]], other.at[place], sems.at[place]
                )
            )
    start(copies)
    wait(copies)


def first_hop(latent, sub_ids, after):
    count = sub_ids.size // CORES
    return pl.pallas_call(
        first_hop_kernel,
        in_specs=[SMEM, ANY, ANY],
        out_specs=VMEM,
        out_shape=blocks_like(count, latent),
        scratch_shapes=[pltpu.SemaphoreType.DMA((count,))],
        compiler_params=params(8),
        name="first_hop",
    )(*map(in_hbm, (sub_ids, latent, after)))


def x_counts(sub_ids):
    slots, peers = sub_ids.shape
    return [slots * CORES] * (peers // CORES - 1)


def pick_kernel(ids, table, out, ids_held, held, staged, load_sems, sems):
    loads = [
        pltpu.make_async_copy(ids, ids_held, load_sems.at[0]),
        pltpu.make_async_copy(table, held, load_sems.at[1]),
    ]
    start(loads)
    wait(loads)
    copies = chunked(staged, out, sems)
    size = staged.shape[0] // len(copies)
    for part, copy in enumerate(copies):
        for slot in range(part * size, (part + 1) * size):
            staged[slot] = held[ids_held[0, slot]]
        copy.start()
    wait(copies)


def pick(coarse, ids):
    shape = (ids.shape[1],) + coarse.shape[1:]
    return pl.pallas_call(
        pick_kernel,
        in_specs=[ANY, ANY],
        out_specs=ANY,
        out_shape=pltpu.HBM(shape, BF16),
        scratch_shapes=[
            pltpu.SMEM(ids.shape, jnp.int32),
            pltpu.VMEM(coarse.shape, BF16),
            pltpu.VMEM(shape, BF16),
            pltpu.SemaphoreType.DMA((2,)),
            pltpu.SemaphoreType.DMA((8,)),
        ],
        compiler_params=params(8),
        name="pick",
    )(in_hbm(ids), in_hbm(coarse))


def repack_kernel(sub_ids, dom_ids, latent, passed, *outs):
    *pieces, up, down = outs
    copy_for_x(latent, sub_ids, passed, pieces)
    copy_for_dom(latent, dom_ids, 0, up)
    copy_for_dom(latent, dom_ids, 1, down)


def repack(latent, passed, sub_ids, dom_ids):
    counts = x_counts(sub_ids) + [dom_ids.shape[1]] * 2
    return pl.pallas_call(
        repack_kernel,
        in_specs=[SMEM, SMEM, VMEM, VMEM],
        out_specs=[VMEM] * len(counts),
        out_shape=[blocks_like(count, latent) for count in counts],
        compiler_params=params(8),
        name="repack",
    )(sub_ids, dom_ids, latent, passed)


def to_other_core(blocks):
    return lax.ppermute(blocks, "sub", [(i, i ^ 1) for i in range(lax.axis_size("sub"))])


def along_x(pieces):
    size = lax.axis_size("sub")
    return [
        lax.ppermute(piece, "sub", [(i, i ^ (way * CORES)) for i in range(size)])
        for way, piece in enumerate(pieces, 1)
    ]


def along_dom(blocks, distance):
    size = lax.axis_size("dom")
    return lax.ppermute(blocks, "dom", [(i, (i + distance) % size) for i in range(size)])


def second_hop(latent, other, sub_ids, dom_ids):
    passed = to_other_core(other)
    *pieces, up, down = repack(latent, passed, sub_ids, dom_ids)
    return [passed, *along_x(pieces), along_dom(up, 1), along_dom(down, -1)]


def fill_pool(pool, own, sub_ids, passed, pieces, below, above):
    slots, peers = sub_ids.shape
    me = lax.axis_index("sub")
    pool[pl.ds(own + (me ^ 1) * slots, slots)] = passed[:slots]
    for way, piece in enumerate(pieces, 1):
        first = own + (me // CORES ^ way) * CORES * slots
        pool[pl.ds(first, piece.shape[0])] = piece[...]
    end = own + peers * slots
    pool[pl.ds(end, below.shape[0])] = below[...]
    pool[pl.ds(end + below.shape[0], above.shape[0])] = above[...]
    clear_ends(pool, below.shape[0])


def copy_to_self(pool, sub_ids, own):
    slots = sub_ids.shape[0]
    me = lax.axis_index("sub")
    for slot in range(slots):
        pool[own + me * slots + slot] = pool[sub_ids[slot, me]]


def clear_ends(pool, count):
    end = pool.shape[0]
    zeros = jnp.zeros((count,) + pool.shape[1:], pool.dtype)

    @pl.when(lax.axis_index("dom") == 0)
    def _():
        pool[pl.ds(end - 2 * count, count)] = zeros

    @pl.when(lax.axis_index("dom") == lax.axis_size("dom") - 1)
    def _():
        pool[pl.ds(end - count, count)] = zeros


def tile_product(weights, table, ids, block, width):
    total = None
    rows = table.shape[1]
    for first in range(0, ids.shape[0], width):
        gathered = jnp.concatenate(
            [table[ids[first + tile, block]] for tile in range(width)], axis=0
        )
        part = jnp.dot(
            weights[block, :, first * rows : (first + width) * rows],
            gathered,
            preferred_element_type=F32,
        )
        total = part if total is None else total + part
    return total.astype(BF16)


def products(weights, table, ids, out, first, last):
    rows = table.shape[1]
    for block in range(first, last):
        out[pl.ds(block * rows, rows)] = tile_product(weights, table, ids, block, 4)


def node_network(hidden, latent, w_out, gain, live):
    hidden = jnp.maximum(hidden, 0.0).astype(BF16)
    out = jnp.dot(hidden, w_out, preferred_element_type=F32)
    average = jnp.mean(out, axis=-1, keepdims=True)
    centred = out - average
    variance = jnp.mean(centred * centred, axis=-1, keepdims=True)
    normed = centred * lax.rsqrt(variance + 1e-05) * gain
    updated = latent.astype(F32) + normed
    return jnp.where(live, updated, 0.0).astype(BF16)


def live_rows(count, first, size):
    return first + lax.broadcasted_iota(jnp.int32, (size, 1), 0) < count


def prepare_kernel(
    slots, received, weights, interp_weights, w_in, b_in, w_out, gain, latent,
    interp, held, pool, *rest,
):
    net, (slots_held, coarse, slots_sem, interp_sems, own_sem, in_sem, network_sems) = rest[:4], rest[4:]
    table = pltpu.make_async_copy(slots, slots_held, slots_sem)
    table.start()
    arriving = chunked(interp_weights, coarse, interp_sems)
    start(arriving)
    blocks = latent.shape[0]
    more = [
        pltpu.make_async_copy(latent, pool.at[pl.ds(0, blocks)], own_sem),
        pltpu.make_async_copy(weights, held, in_sem),
    ]
    more += [
        pltpu.make_async_copy(source, target, network_sems.at[position])
        for position, (source, target) in enumerate(zip((w_in, b_in, w_out, gain), net))
    ]
    table.wait()
    size = blocks // len(arriving)
    for part, copy in enumerate(arriving):
        copy.wait()
        if part == 0:
            start(more)
        products(coarse, received, slots_held, interp, part * size, (part + 1) * size)
    wait(more)


def prepare(received, slots, interp_weights, latent, pool, weights, network):
    blocks, rows, lat = latent.shape
    return pl.pallas_call(
        prepare_kernel,
        in_specs=[ANY, VMEM] + [ANY] * 7,
        out_specs=[VMEM] * 7,
        out_shape=[
            jax.ShapeDtypeStruct((blocks * rows, lat), BF16),
            pltpu.VMEM(weights.shape, BF16),
            pltpu.VMEM((pool, rows, lat), BF16),
            *(pltpu.VMEM(part.shape, part.dtype) for part in network),
        ],
        scratch_shapes=[
            pltpu.SMEM(slots.shape, jnp.int32),
            pltpu.VMEM(interp_weights.shape, BF16),
            pltpu.SemaphoreType.DMA,
            pltpu.SemaphoreType.DMA((2,)),
            pltpu.SemaphoreType.DMA,
            pltpu.SemaphoreType.DMA,
            pltpu.SemaphoreType.DMA((4,)),
        ],
        compiler_params=params(8),
        name="prepare",
    )(in_hbm(slots), received, *map(in_hbm, (weights, interp_weights, *network, latent)))


def first_kernel(
    count, ids, sub_ids, weights, interp, w_in, b_in, w_out, gain, pool_in, passed, *rest
):
    del pool_in
    ways = sub_ids.shape[1] // CORES - 1
    pieces, (below, above, pool, other, summed) = rest[:ways], rest[ways:]
    blocks = weights.shape[0]
    rows, lat = pool.shape[1:]
    fill_pool(pool, blocks, sub_ids, passed, pieces, below, above)
    copy_to_self(pool, sub_ids, blocks)
    products(weights, pool, ids, summed, 0, blocks)
    own = pool[pl.ds(0, blocks)].reshape(blocks * rows, lat)
    joined = jnp.concatenate([own, summed[...], interp[...]], axis=1)
    hidden = jnp.dot(joined, w_in[0], preferred_element_type=F32) + b_in[0:1]
    live = live_rows(count[0] * rows, 0, blocks * rows)
    new = node_network(hidden, own, w_out[0], gain[0:1], live)
    pool[pl.ds(0, blocks)] = new.reshape(blocks, rows, lat)
    copy_for_other_core(pool, sub_ids, other)
    copy_to_self(pool, sub_ids, blocks)


def first_step(pool, halo, weights, interp, ids, network, count, sub_ids):
    rows, lat = pool.shape[1:]
    blocks = weights.shape[0]
    operands = [count, ids, sub_ids, *map(in_vmem, (weights, interp, *network, pool))]
    return pl.pallas_call(
        first_kernel,
        in_specs=[SMEM] * 3 + [VMEM] * (7 + len(halo)),
        out_specs=[VMEM] * 2,
        out_shape=[
            pltpu.VMEM(pool.shape, BF16),
            jax.ShapeDtypeStruct((sub_ids.size // CORES, rows, lat), BF16),
        ],
        input_output_aliases={len(operands) - 1: 0},
        scratch_shapes=[pltpu.VMEM((blocks * rows, lat), BF16)],
        compiler_params=params(16),
        name="first_step",
    )(*operands, *halo)


def second_kernel(
    ids, count, weights, interp, w_in, b_in, w_out, gain, pool_in, sub_shape, passed, *rest
):
    del pool_in
    ways = sub_shape.shape[1] // CORES - 1
    pieces, (below, above, *rest) = rest[:ways], rest[ways:]
    pool, out, summed, staged, out_sems = rest
    blocks, rows, lat = staged.shape
    fill_pool(pool, blocks, sub_shape, passed, pieces, below, above)
    products(weights, pool, ids, summed, 0, blocks)
    copies = chunked(staged, out, out_sems)
    size = blocks // len(copies)
    for part, copy in enumerate(copies):
        mine = pl.ds(part * size, size)
        here = pl.ds(part * size * rows, size * rows)
        own = pool[mine].reshape(size * rows, lat)
        joined = jnp.concatenate([own, summed[here], interp[here]], axis=1)
        hidden = jnp.dot(joined, w_in[1], preferred_element_type=F32) + b_in[1:2]
        live = live_rows(count[0] * rows, part * size * rows, size * rows)
        new = node_network(hidden, own, w_out[1], gain[1:2], live)
        staged[mine] = new.reshape(size, rows, lat)
        copy.start()
    wait(copies)


def second_step(pool, halo, weights, interp, ids, network, count, sub_ids):
    rows, lat = pool.shape[1:]
    blocks = weights.shape[0]
    operands = [ids, count, *map(in_vmem, (weights, interp, *network, pool))]
    return pl.pallas_call(
        second_kernel,
        in_specs=[SMEM] * 2 + [VMEM] * 7 + [ANY] + [VMEM] * len(halo),
        out_specs=[VMEM, ANY],
        out_shape=[pltpu.VMEM(pool.shape, BF16), pltpu.HBM((blocks, rows, lat), BF16)],
        input_output_aliases={len(operands) - 1: 0},
        scratch_shapes=[
            pltpu.VMEM((blocks * rows, lat), BF16),
            pltpu.VMEM((blocks, rows, lat), BF16),
            pltpu.SemaphoreType.DMA((2,)),
        ],
        compiler_params=params(16),
        name="second_step",
    )(*operands, sub_ids, *halo)[1]


def per_device(
    fine_latent,
    coarse_latent,
    adj_index,
    adj_weight,
    interp_slot,
    interp_weight,
    coarse_send,
    halo_sub_send,
    halo_dom_send,
    block_count,
    w_in,
    b_in,
    w_out,
    ln_gain,
):
    sub_ids = halo_sub_send[0].T
    dom_ids = halo_dom_send[0]
    adj_ids = adj_index.T
    payload = pick(coarse_latent, coarse_send.reshape(1, -1))
    received = lax.all_to_all(payload, ("dom", "sub"), split_axis=0, concat_axis=0, tiled=True)
    halo = second_hop(fine_latent, first_hop(fine_latent, sub_ids, payload), sub_ids, dom_ids)
    size = fine_latent.shape[0] + sub_ids.size + dom_ids.size
    interp, weights, pool, *network = prepare(
        received, interp_slot.T, interp_weight, fine_latent, size, adj_weight,
        (w_in, b_in, w_out, ln_gain),
    )
    pool, other = first_step(pool, halo, weights, interp, adj_ids, network, block_count, sub_ids)
    halo = second_hop(pool, other, sub_ids, dom_ids)
    return second_step(pool, halo, weights, interp, adj_ids, network, block_count, sub_ids)


def solution(mesh):
    split = ("dom", "sub")
    placed = (
        P(split, None, None),
        P(split, None, None),
        P(split, None),
        P(split, None, None),
        P(split, None),
        P(split, None, None),
        P(split, None, None),
        P(split, None, None),
        P(split, None, None),
        P(split),
        P(),
        P(),
        P(),
        P(),
    )
    return jax.shard_map(
        per_device,
        mesh=mesh,
        in_specs=placed,
        out_specs=P(split, None, None),
        check_vma=False,
    )
```

```python
import functools

import jax
import jax.numpy as jnp
from jax import lax
from jax.experimental import pallas as pl
from jax.experimental.pallas import tpu as pltpu
from jax.sharding import PartitionSpec as P

BF16 = jnp.bfloat16
F32 = jnp.float32
SMEM = pl.BlockSpec(memory_space=pltpu.SMEM)
VMEM = pl.BlockSpec(memory_space=pltpu.VMEM)
ANY = pl.BlockSpec(memory_space=pl.ANY)
CORES = 2


def in_hbm(array):
    return pltpu.with_memory_space_constraint(array, pltpu.HBM)


def in_vmem(array):
    return pltpu.with_memory_space_constraint(array, pltpu.VMEM)


def params(mib):
    return pltpu.CompilerParams(vmem_limit_bytes=mib << 20)


def blocks_like(count, latent):
    return jax.ShapeDtypeStruct((count,) + latent.shape[1:], BF16)


def chunked(source, target, sems):
    parts = sems.shape[0]
    size = source.shape[0] // parts
    return [
        pltpu.make_async_copy(
            source.at[pl.ds(part * size, size)], target.at[pl.ds(part * size, size)], sems.at[part]
        )
        for part in range(parts)
    ]


def start(copies):
    for copy in copies:
        copy.start()


def wait(copies):
    for copy in copies:
        copy.wait()


def copy_for_other_core(latent, sub_ids, out):
    slots, peers = sub_ids.shape
    me = lax.axis_index("sub")
    for way in range(peers // CORES):
        peer = me ^ (way * CORES + 1)
        for slot in range(slots):
            out[way * slots + slot] = latent[sub_ids[slot, peer]]


def copy_for_dom(latent, dom_ids, way, out):
    for slot in range(dom_ids.shape[1]):
        out[slot] = latent[dom_ids[way, slot]]


def copy_for_x(latent, sub_ids, passed, outs):
    slots = sub_ids.shape[0]
    me = lax.axis_index("sub")
    mine = (me % CORES) * slots
    for way, out in enumerate(outs, 1):
        for slot in range(slots):
            out[mine + slot] = latent[sub_ids[slot, me ^ (way * CORES)]]
            out[slots - mine + slot] = passed[way * slots + slot]


def first_hop_kernel(sub_ids, latent, after, other, sems):
    del after
    slots, peers = sub_ids.shape
    me = lax.axis_index("sub")
    copies = []
    for way in range(peers // CORES):
        peer = me ^ (way * CORES + 1)
        for slot in range(slots):
            place = way * slots + slot
            copies.append(
                pltpu.make_async_copy(
                    latent.at[sub_ids[slot, peer]], other.at[place], sems.at[place]
                )
            )
    start(copies)
    wait(copies)


def first_hop(latent, sub_ids, after):
    count = sub_ids.size // CORES
    return pl.pallas_call(
        first_hop_kernel,
        in_specs=[SMEM, ANY, ANY],
        out_specs=VMEM,
        out_shape=blocks_like(count, latent),
        scratch_shapes=[pltpu.SemaphoreType.DMA((count,))],
        compiler_params=params(8),
        name="first_hop",
    )(*map(in_hbm, (sub_ids, latent, after)))


def x_counts(sub_ids):
    slots, peers = sub_ids.shape
    return [slots * CORES] * (peers // CORES - 1)


def pick_kernel(ids, table, out, ids_held, held, staged, load_sems, sems):
    loads = [
        pltpu.make_async_copy(ids, ids_held, load_sems.at[0]),
        pltpu.make_async_copy(table, held, load_sems.at[1]),
    ]
    start(loads)
    wait(loads)
    copies = chunked(staged, out, sems)
    size = staged.shape[0] // len(copies)
    for part, copy in enumerate(copies):
        for slot in range(part * size, (part + 1) * size):
            staged[slot] = held[ids_held[0, slot]]
        copy.start()
    wait(copies)


def pick(coarse, ids):
    shape = (ids.shape[1],) + coarse.shape[1:]
    return pl.pallas_call(
        pick_kernel,
        in_specs=[ANY, ANY],
        out_specs=ANY,
        out_shape=pltpu.HBM(shape, BF16),
        scratch_shapes=[
            pltpu.SMEM(ids.shape, jnp.int32),
            pltpu.VMEM(coarse.shape, BF16),
            pltpu.VMEM(shape, BF16),
            pltpu.SemaphoreType.DMA((2,)),
            pltpu.SemaphoreType.DMA((8,)),
        ],
        compiler_params=params(8),
        name="pick",
    )(in_hbm(ids), in_hbm(coarse))


def repack_kernel(sub_ids, dom_ids, latent, passed, *outs):
    *pieces, up, down = outs
    copy_for_x(latent, sub_ids, passed, pieces)
    copy_for_dom(latent, dom_ids, 0, up)
    copy_for_dom(latent, dom_ids, 1, down)


def repack(latent, passed, sub_ids, dom_ids):
    counts = x_counts(sub_ids) + [dom_ids.shape[1]] * 2
    return pl.pallas_call(
        repack_kernel,
        in_specs=[SMEM, SMEM, VMEM, VMEM],
        out_specs=[VMEM] * len(counts),
        out_shape=[blocks_like(count, latent) for count in counts],
        compiler_params=params(8),
        name="repack",
    )(sub_ids, dom_ids, latent, passed)


def to_other_core(blocks):
    return lax.ppermute(blocks, "sub", [(i, i ^ 1) for i in range(lax.axis_size("sub"))])


def along_x(pieces):
    size = lax.axis_size("sub")
    return [
        lax.ppermute(piece, "sub", [(i, i ^ (way * CORES)) for i in range(size)])
        for way, piece in enumerate(pieces, 1)
    ]


def along_dom(blocks, distance):
    size = lax.axis_size("dom")
    return lax.ppermute(blocks, "dom", [(i, (i + distance) % size) for i in range(size)])


def second_hop(latent, other, sub_ids, dom_ids):
    passed = to_other_core(other)
    *pieces, up, down = repack(latent, passed, sub_ids, dom_ids)
    return [passed, *along_x(pieces), along_dom(up, 1), along_dom(down, -1)]


def fill_pool(pool, own, sub_ids, passed, pieces, below, above):
    slots, peers = sub_ids.shape
    me = lax.axis_index("sub")
    pool[pl.ds(own + (me ^ 1) * slots, slots)] = passed[:slots]
    for way, piece in enumerate(pieces, 1):
        first = own + (me // CORES ^ way) * CORES * slots
        pool[pl.ds(first, piece.shape[0])] = piece[...]
    end = own + peers * slots
    pool[pl.ds(end, below.shape[0])] = below[...]
    pool[pl.ds(end + below.shape[0], above.shape[0])] = above[...]
    clear_ends(pool, below.shape[0])


def copy_to_self(pool, sub_ids, own):
    slots = sub_ids.shape[0]
    me = lax.axis_index("sub")
    for slot in range(slots):
        pool[own + me * slots + slot] = pool[sub_ids[slot, me]]


def clear_ends(pool, count):
    end = pool.shape[0]
    zeros = jnp.zeros((count,) + pool.shape[1:], pool.dtype)

    @pl.when(lax.axis_index("dom") == 0)
    def _():
        pool[pl.ds(end - 2 * count, count)] = zeros

    @pl.when(lax.axis_index("dom") == lax.axis_size("dom") - 1)
    def _():
        pool[pl.ds(end - count, count)] = zeros


def tile_product(weights, table, ids, block, width):
    total = None
    rows = table.shape[1]
    for first in range(0, ids.shape[0], width):
        gathered = jnp.concatenate(
            [table[ids[first + tile, block]] for tile in range(width)], axis=0
        )
        part = jnp.dot(
            weights[block, :, first * rows : (first + width) * rows],
            gathered,
            preferred_element_type=F32,
        )
        total = part if total is None else total + part
    return total.astype(BF16)


def products(weights, table, ids, out, first, last):
    rows = table.shape[1]
    for block in range(first, last):
        out[pl.ds(block * rows, rows)] = tile_product(weights, table, ids, block, 4)


def node_network(hidden, latent, w_out, gain, live):
    hidden = jnp.maximum(hidden, 0.0).astype(BF16)
    out = jnp.dot(hidden, w_out, preferred_element_type=F32)
    average = jnp.mean(out, axis=-1, keepdims=True)
    centred = out - average
    variance = jnp.mean(centred * centred, axis=-1, keepdims=True)
    normed = centred * lax.rsqrt(variance + 1e-05) * gain
    updated = latent.astype(F32) + normed
    return jnp.where(live, updated, 0.0).astype(BF16)


def live_rows(count, first, size):
    return first + lax.broadcasted_iota(jnp.int32, (size, 1), 0) < count


def prepare_kernel(
    slots, received, weights, interp_weights, w_in, b_in, w_out, gain, latent,
    interp, held, pool, *rest,
):
    net, (slots_held, coarse, slots_sem, interp_sems, own_sem, in_sem, network_sems) = rest[:4], rest[4:]
    table = pltpu.make_async_copy(slots, slots_held, slots_sem)
    table.start()
    arriving = chunked(interp_weights, coarse, interp_sems)
    start(arriving)
    blocks = latent.shape[0]
    more = [
        pltpu.make_async_copy(latent, pool.at[pl.ds(0, blocks)], own_sem),
        pltpu.make_async_copy(weights, held, in_sem),
    ]
    more += [
        pltpu.make_async_copy(source, target, network_sems.at[position])
        for position, (source, target) in enumerate(zip((w_in, b_in, w_out, gain), net))
    ]
    table.wait()
    size = blocks // len(arriving)
    for part, copy in enumerate(arriving):
        copy.wait()
        if part == 0:
            start(more)
        products(coarse, received, slots_held, interp, part * size, (part + 1) * size)
    wait(more)


def prepare(received, slots, interp_weights, latent, pool, weights, network):
    blocks, rows, lat = latent.shape
    return pl.pallas_call(
        prepare_kernel,
        in_specs=[ANY, VMEM] + [ANY] * 7,
        out_specs=[VMEM] * 7,
        out_shape=[
            jax.ShapeDtypeStruct((blocks * rows, lat), BF16),
            pltpu.VMEM(weights.shape, BF16),
            pltpu.VMEM((pool, rows, lat), BF16),
            *(pltpu.VMEM(part.shape, part.dtype) for part in network),
        ],
        scratch_shapes=[
            pltpu.SMEM(slots.shape, jnp.int32),
            pltpu.VMEM(interp_weights.shape, BF16),
            pltpu.SemaphoreType.DMA,
            pltpu.SemaphoreType.DMA((2,)),
            pltpu.SemaphoreType.DMA,
            pltpu.SemaphoreType.DMA,
            pltpu.SemaphoreType.DMA((4,)),
        ],
        compiler_params=params(8),
        name="prepare",
    )(in_hbm(slots), received, *map(in_hbm, (weights, interp_weights, *network, latent)))


def first_kernel(
    count, ids, sub_ids, weights, interp, w_in, b_in, w_out, gain, pool_in, passed, *rest
):
    del pool_in
    ways = sub_ids.shape[1] // CORES - 1
    pieces, (below, above, pool, other, summed) = rest[:ways], rest[ways:]
    blocks = weights.shape[0]
    rows, lat = pool.shape[1:]
    fill_pool(pool, blocks, sub_ids, passed, pieces, below, above)
    copy_to_self(pool, sub_ids, blocks)
    products(weights, pool, ids, summed, 0, blocks)
    own = pool[pl.ds(0, blocks)].reshape(blocks * rows, lat)
    joined = jnp.concatenate([own, summed[...], interp[...]], axis=1)
    hidden = jnp.dot(joined, w_in[0], preferred_element_type=F32) + b_in[0:1]
    live = live_rows(count[0] * rows, 0, blocks * rows)
    new = node_network(hidden, own, w_out[0], gain[0:1], live)
    pool[pl.ds(0, blocks)] = new.reshape(blocks, rows, lat)
    copy_for_other_core(pool, sub_ids, other)
    copy_to_self(pool, sub_ids, blocks)


def first_step(pool, halo, weights, interp, ids, network, count, sub_ids):
    rows, lat = pool.shape[1:]
    blocks = weights.shape[0]
    operands = [count, ids, sub_ids, *map(in_vmem, (weights, interp, *network, pool))]
    return pl.pallas_call(
        first_kernel,
        in_specs=[SMEM] * 3 + [VMEM] * (7 + len(halo)),
        out_specs=[VMEM] * 2,
        out_shape=[
            pltpu.VMEM(pool.shape, BF16),
            jax.ShapeDtypeStruct((sub_ids.size // CORES, rows, lat), BF16),
        ],
        input_output_aliases={len(operands) - 1: 0},
        scratch_shapes=[pltpu.VMEM((blocks * rows, lat), BF16)],
        compiler_params=params(16),
        name="first_step",
    )(*operands, *halo)


def second_kernel(
    ids, count, weights, interp, w_in, b_in, w_out, gain, pool_in, sub_shape, passed, *rest
):
    del pool_in
    ways = sub_shape.shape[1] // CORES - 1
    last, below, above, *rest = rest
    pieces, rest = [*rest[: ways - 1], last], rest[ways - 1 :]
    pool, out, summed, staged, out_sems = rest
    blocks, rows, lat = staged.shape
    fill_pool(pool, blocks, sub_shape, passed, pieces, below, above)
    products(weights, pool, ids, summed, 0, blocks)
    copies = chunked(staged, out, out_sems)
    size = blocks // len(copies)
    for part, copy in enumerate(copies):
        mine = pl.ds(part * size, size)
        here = pl.ds(part * size * rows, size * rows)
        own = pool[mine].reshape(size * rows, lat)
        joined = jnp.concatenate([own, summed[here], interp[here]], axis=1)
        hidden = jnp.dot(joined, w_in[1], preferred_element_type=F32) + b_in[1:2]
        live = live_rows(count[0] * rows, part * size * rows, size * rows)
        new = node_network(hidden, own, w_out[1], gain[1:2], live)
        staged[mine] = new.reshape(size, rows, lat)
        copy.start()
    wait(copies)


def second_step(pool, halo, weights, interp, ids, network, count, sub_ids):
    rows, lat = pool.shape[1:]
    blocks = weights.shape[0]
    passed, *pieces, below, above = halo
    operands = [ids, count, *map(in_vmem, (weights, interp, *network, pool))]
    return pl.pallas_call(
        second_kernel,
        in_specs=[SMEM] * 2 + [VMEM] * 7 + [ANY] + [VMEM] * len(halo),
        out_specs=[VMEM, ANY],
        out_shape=[pltpu.VMEM(pool.shape, BF16), pltpu.HBM((blocks, rows, lat), BF16)],
        input_output_aliases={len(operands) - 1: 0},
        scratch_shapes=[
            pltpu.VMEM((blocks * rows, lat), BF16),
            pltpu.VMEM((blocks, rows, lat), BF16),
            pltpu.SemaphoreType.DMA((2,)),
        ],
        compiler_params=params(16),
        name="second_step",
    )(*operands, sub_ids, passed, *pieces[-1:], below, above, *pieces[:-1])[1]


def per_device(
    fine_latent,
    coarse_latent,
    adj_index,
    adj_weight,
    interp_slot,
    interp_weight,
    coarse_send,
    halo_sub_send,
    halo_dom_send,
    block_count,
    w_in,
    b_in,
    w_out,
    ln_gain,
):
    sub_ids = halo_sub_send[0].T
    dom_ids = halo_dom_send[0]
    adj_ids = adj_index.T
    payload = pick(coarse_latent, coarse_send.reshape(1, -1))
    received = lax.all_to_all(payload, ("dom", "sub"), split_axis=0, concat_axis=0, tiled=True)
    halo = second_hop(fine_latent, first_hop(fine_latent, sub_ids, payload), sub_ids, dom_ids)
    size = fine_latent.shape[0] + sub_ids.size + dom_ids.size
    interp, weights, pool, *network = prepare(
        received, interp_slot.T, interp_weight, fine_latent, size, adj_weight,
        (w_in, b_in, w_out, ln_gain),
    )
    pool, other = first_step(pool, halo, weights, interp, adj_ids, network, block_count, sub_ids)
    halo = second_hop(pool, other, sub_ids, dom_ids)
    return second_step(pool, halo, weights, interp, adj_ids, network, block_count, sub_ids)


def solution(mesh):
    split = ("dom", "sub")
    placed = (
        P(split, None, None),
        P(split, None, None),
        P(split, None),
        P(split, None, None),
        P(split, None),
        P(split, None, None),
        P(split, None, None),
        P(split, None, None),
        P(split, None, None),
        P(split),
        P(),
        P(),
        P(),
        P(),
    )
    return jax.shard_map(
        per_device,
        mesh=mesh,
        in_specs=placed,
        out_specs=P(split, None, None),
        check_vma=False,
    )
```

```python
import functools

import jax
import jax.numpy as jnp
from jax import lax
from jax.experimental import pallas as pl
from jax.experimental.pallas import tpu as pltpu
from jax.sharding import PartitionSpec as P

BF16 = jnp.bfloat16
F32 = jnp.float32
SMEM = pl.BlockSpec(memory_space=pltpu.SMEM)
VMEM = pl.BlockSpec(memory_space=pltpu.VMEM)
ANY = pl.BlockSpec(memory_space=pl.ANY)
CORES = 2
WAYS = (1, 3, 2)
AHEAD = 2


def in_hbm(array):
    return pltpu.with_memory_space_constraint(array, pltpu.HBM)


def in_vmem(array):
    return pltpu.with_memory_space_constraint(array, pltpu.VMEM)


def params(mib):
    return pltpu.CompilerParams(vmem_limit_bytes=mib << 20)


def blocks_like(count, latent):
    return jax.ShapeDtypeStruct((count,) + latent.shape[1:], BF16)


def chunked(source, target, sems):
    parts = sems.shape[0]
    size = source.shape[0] // parts
    return [
        pltpu.make_async_copy(
            source.at[pl.ds(part * size, size)], target.at[pl.ds(part * size, size)], sems.at[part]
        )
        for part in range(parts)
    ]


def start(copies):
    for copy in copies:
        copy.start()


def wait(copies):
    for copy in copies:
        copy.wait()


def copy_for_other_core(latent, sub_ids, out):
    slots, peers = sub_ids.shape
    me = lax.axis_index("sub")
    for way in range(peers // CORES):
        peer = me ^ (way * CORES + 1)
        for slot in range(slots):
            out[way * slots + slot] = latent[sub_ids[slot, peer]]


def copy_for_dom(latent, dom_ids, way, out):
    for slot in range(dom_ids.shape[1]):
        out[slot] = latent[dom_ids[way, slot]]


def copy_for_x(latent, sub_ids, passed, outs):
    slots = sub_ids.shape[0]
    me = lax.axis_index("sub")
    mine = (me % CORES) * slots
    for way, out in zip(WAYS, outs):
        for slot in range(slots):
            out[mine + slot] = latent[sub_ids[slot, me ^ (way * CORES)]]
            out[slots - mine + slot] = passed[way * slots + slot]


def first_hop_kernel(sub_ids, latent, after, other, sems):
    del after
    slots, peers = sub_ids.shape
    me = lax.axis_index("sub")
    copies = []
    for way in range(peers // CORES):
        peer = me ^ (way * CORES + 1)
        for slot in range(slots):
            place = way * slots + slot
            copies.append(
                pltpu.make_async_copy(
                    latent.at[sub_ids[slot, peer]], other.at[place], sems.at[place]
                )
            )
    start(copies)
    wait(copies)


def first_hop(latent, sub_ids, after):
    count = sub_ids.size // CORES
    return pl.pallas_call(
        first_hop_kernel,
        in_specs=[SMEM, ANY, ANY],
        out_specs=VMEM,
        out_shape=blocks_like(count, latent),
        scratch_shapes=[pltpu.SemaphoreType.DMA((count,))],
        compiler_params=params(8),
        name="first_hop",
    )(*map(in_hbm, (sub_ids, latent, after)))


def x_counts(sub_ids):
    slots, peers = sub_ids.shape
    return [slots * CORES] * (peers // CORES - 1)


def pick_kernel(ids, table, out, ids_held, held, staged, load_sems, sems):
    loads = [
        pltpu.make_async_copy(ids, ids_held, load_sems.at[0]),
        pltpu.make_async_copy(table, held, load_sems.at[1]),
    ]
    start(loads)
    wait(loads)
    copies = chunked(staged, out, sems)
    size = staged.shape[0] // len(copies)
    for part, copy in enumerate(copies):
        for slot in range(part * size, (part + 1) * size):
            staged[slot] = held[ids_held[0, slot]]
        copy.start()
    wait(copies)


def pick(coarse, ids):
    shape = (ids.shape[1],) + coarse.shape[1:]
    return pl.pallas_call(
        pick_kernel,
        in_specs=[ANY, ANY],
        out_specs=ANY,
        out_shape=pltpu.HBM(shape, BF16),
        scratch_shapes=[
            pltpu.SMEM(ids.shape, jnp.int32),
            pltpu.VMEM(coarse.shape, BF16),
            pltpu.VMEM(shape, BF16),
            pltpu.SemaphoreType.DMA((2,)),
            pltpu.SemaphoreType.DMA((8,)),
        ],
        compiler_params=params(8),
        name="pick",
    )(in_hbm(ids), in_hbm(coarse))


def repack_kernel(sub_ids, dom_ids, latent, passed, *outs):
    *pieces, up, down = outs
    copy_for_x(latent, sub_ids, passed, pieces)
    copy_for_dom(latent, dom_ids, 0, up)
    copy_for_dom(latent, dom_ids, 1, down)


def repack(latent, passed, sub_ids, dom_ids):
    counts = x_counts(sub_ids) + [dom_ids.shape[1]] * 2
    return pl.pallas_call(
        repack_kernel,
        in_specs=[SMEM, SMEM, VMEM, VMEM],
        out_specs=[VMEM] * len(counts),
        out_shape=[blocks_like(count, latent) for count in counts],
        compiler_params=params(8),
        name="repack",
    )(sub_ids, dom_ids, latent, passed)


def to_other_core(blocks):
    return lax.ppermute(blocks, "sub", [(i, i ^ 1) for i in range(lax.axis_size("sub"))])


def along_x(pieces):
    size = lax.axis_size("sub")
    return [
        lax.ppermute(piece, "sub", [(i, i ^ (way * CORES)) for i in range(size)])
        for way, piece in zip(WAYS, pieces)
    ]


def along_dom(blocks, distance):
    size = lax.axis_size("dom")
    return lax.ppermute(blocks, "dom", [(i, (i + distance) % size) for i in range(size)])


def second_hop(latent, other, sub_ids, dom_ids):
    passed = to_other_core(other)
    *pieces, up, down = repack(latent, passed, sub_ids, dom_ids)
    return [passed, *along_x(pieces), along_dom(up, 1), along_dom(down, -1)]


def fill_pool(pool, own, sub_ids, passed, pieces, below, above):
    slots, peers = sub_ids.shape
    me = lax.axis_index("sub")
    pool[pl.ds(own + (me ^ 1) * slots, slots)] = passed[:slots]
    for way, piece in zip(WAYS, pieces):
        first = own + (me // CORES ^ way) * CORES * slots
        pool[pl.ds(first, piece.shape[0])] = piece[...]
    end = own + peers * slots
    pool[pl.ds(end, below.shape[0])] = below[...]
    pool[pl.ds(end + below.shape[0], above.shape[0])] = above[...]
    clear_ends(pool, below.shape[0])


def copy_to_self(pool, sub_ids, own):
    slots = sub_ids.shape[0]
    me = lax.axis_index("sub")
    for slot in range(slots):
        pool[own + me * slots + slot] = pool[sub_ids[slot, me]]


def clear_ends(pool, count):
    end = pool.shape[0]
    zeros = jnp.zeros((count,) + pool.shape[1:], pool.dtype)

    @pl.when(lax.axis_index("dom") == 0)
    def _():
        pool[pl.ds(end - 2 * count, count)] = zeros

    @pl.when(lax.axis_index("dom") == lax.axis_size("dom") - 1)
    def _():
        pool[pl.ds(end - count, count)] = zeros


def tile_product(weights, table, ids, block, width):
    total = None
    rows = table.shape[1]
    for first in range(0, ids.shape[0], width):
        gathered = jnp.concatenate(
            [table[ids[first + tile, block]] for tile in range(width)], axis=0
        )
        part = jnp.dot(
            weights[block, :, first * rows : (first + width) * rows],
            gathered,
            preferred_element_type=F32,
        )
        total = part if total is None else total + part
    return total.astype(BF16)


def products(weights, table, ids, out, first, last):
    rows = table.shape[1]
    for block in range(first, last):
        out[pl.ds(block * rows, rows)] = tile_product(weights, table, ids, block, 4)


def node_network(hidden, latent, w_out, gain, live):
    hidden = jnp.maximum(hidden, 0.0).astype(BF16)
    out = jnp.dot(hidden, w_out, preferred_element_type=F32)
    average = jnp.mean(out, axis=-1, keepdims=True)
    centred = out - average
    variance = jnp.mean(centred * centred, axis=-1, keepdims=True)
    normed = centred * lax.rsqrt(variance + 1e-05) * gain
    updated = latent.astype(F32) + normed
    return jnp.where(live, updated, 0.0).astype(BF16)


def live_rows(count, first, size):
    return first + lax.broadcasted_iota(jnp.int32, (size, 1), 0) < count


def first_kernel(
    count, ids, sub_ids, slots, received, weights, interp_weights, w_in, b_in, w_out, gain, latent,
    passed, *rest,
):
    ways = sub_ids.shape[1] // CORES - 1
    pieces, (below, above, *rest) = rest[:ways], rest[ways:]
    pool, other, interp, held, summed, coarse, *rest = rest
    tables, net, sems = rest[:3], rest[3:7], rest[7:]
    table_sems, interp_sems, own_sem, in_sems, network_sems = sems
    tabling = [
        pltpu.make_async_copy(source, target, table_sems.at[position])
        for position, (source, target) in enumerate(zip((slots, sub_ids, ids), tables))
    ]
    start(tabling)
    slots, sub_ids, ids = tables
    coarse_arriving = chunked(interp_weights, coarse, interp_sems)
    arriving = chunked(weights, held, in_sems)
    blocks, rows, lat = latent.shape
    bring = pltpu.make_async_copy(latent, pool.at[pl.ds(0, blocks)], own_sem)
    network = [
        pltpu.make_async_copy(source, target, network_sems.at[position])
        for position, (source, target) in enumerate(zip((w_in, b_in, w_out, gain), net))
    ]
    start(coarse_arriving)
    bring.start()
    queue = arriving + network
    start(queue[:AHEAD])
    queue = queue[AHEAD:]
    w_in, b_in, w_out, gain = net
    wait(tabling)
    fill_pool(pool, blocks, sub_ids, passed, pieces, below, above)
    size = blocks // len(coarse_arriving)
    for part, copy in enumerate(coarse_arriving):
        copy.wait()
        start(queue[:1])
        queue = queue[1:]
        products(coarse, received, slots, interp, part * size, (part + 1) * size)
    bring.wait()
    copy_to_self(pool, sub_ids, blocks)
    size = blocks // len(arriving)
    for part, copy in enumerate(arriving):
        copy.wait()
        start(queue[:2])
        queue = queue[2:]
        products(held, pool, ids, summed, part * size, (part + 1) * size)
    start(queue)
    wait(network)
    own = pool[pl.ds(0, blocks)].reshape(blocks * rows, lat)
    joined = jnp.concatenate([own, summed[...], interp[...]], axis=1)
    hidden = jnp.dot(joined, w_in[0], preferred_element_type=F32) + b_in[0:1]
    live = live_rows(count[0] * rows, 0, blocks * rows)
    new = node_network(hidden, own, w_out[0], gain[0:1], live)
    pool[pl.ds(0, blocks)] = new.reshape(blocks, rows, lat)
    copy_for_other_core(pool, sub_ids, other)
    copy_to_self(pool, sub_ids, blocks)


def first_step(
    received, slots, interp_weights, latent, halo, ids, weights, w_in, b_in, w_out, gain, count,
    sub_ids,
):
    blocks, rows, lat = latent.shape
    pool = blocks + sub_ids.size + 2 * halo[-1].shape[0]
    network = (w_in, b_in, w_out, gain)
    return pl.pallas_call(
        first_kernel,
        in_specs=[SMEM, ANY, ANY, ANY, VMEM] + [ANY] * 7 + [VMEM] * len(halo),
        out_specs=[VMEM] * 4,
        out_shape=[
            pltpu.VMEM((pool, rows, lat), BF16),
            blocks_like(sub_ids.size // CORES, latent),
            jax.ShapeDtypeStruct((blocks * rows, lat), BF16),
            pltpu.VMEM(weights.shape, BF16),
        ],
        scratch_shapes=[
            pltpu.VMEM((blocks * rows, lat), BF16),
            pltpu.VMEM(interp_weights.shape, BF16),
            *(pltpu.SMEM(part.shape, jnp.int32) for part in (slots, sub_ids, ids)),
            *(pltpu.VMEM(part.shape, part.dtype) for part in network),
            pltpu.SemaphoreType.DMA((3,)),
            pltpu.SemaphoreType.DMA((2,)),
            pltpu.SemaphoreType.DMA,
            pltpu.SemaphoreType.DMA((4,)),
            pltpu.SemaphoreType.DMA((4,)),
        ],
        compiler_params=params(16),
        name="first_step",
    )(
        count, *map(in_hbm, (ids, sub_ids, slots)), received,
        *map(in_hbm, (weights, interp_weights, *network, latent)), *halo,
    )


def second_kernel(
    ids, count, weights, interp, w_in, b_in, w_out, gain, pool_in, sub_shape, passed, *rest
):
    del pool_in
    ways = sub_shape.shape[1] // CORES - 1
    pieces, (below, above, *rest) = rest[:ways], rest[ways:]
    pool, out, summed, staged, out_sems = rest
    blocks, rows, lat = staged.shape
    fill_pool(pool, blocks, sub_shape, passed, pieces, below, above)
    products(weights, pool, ids, summed, 0, blocks)
    copies = chunked(staged, out, out_sems)
    size = blocks // len(copies)
    for part, copy in enumerate(copies):
        mine = pl.ds(part * size, size)
        here = pl.ds(part * size * rows, size * rows)
        own = pool[mine].reshape(size * rows, lat)
        joined = jnp.concatenate([own, summed[here], interp[here]], axis=1)
        hidden = jnp.dot(joined, w_in[1], preferred_element_type=F32) + b_in[1:2]
        live = live_rows(count[0] * rows, part * size * rows, size * rows)
        new = node_network(hidden, own, w_out[1], gain[1:2], live)
        staged[mine] = new.reshape(size, rows, lat)
        copy.start()
    wait(copies)


def second_step(pool, halo, weights, interp, ids, w_in, b_in, w_out, gain, count, sub_ids):
    rows, lat = pool.shape[1:]
    blocks = weights.shape[0]
    operands = [ids, count, in_vmem(weights), interp, w_in, b_in, w_out, gain, in_vmem(pool)]
    return pl.pallas_call(
        second_kernel,
        in_specs=[SMEM] * 2 + [VMEM] * 7 + [ANY] + [VMEM] * len(halo),
        out_specs=[VMEM, ANY],
        out_shape=[pltpu.VMEM(pool.shape, BF16), pltpu.HBM((blocks, rows, lat), BF16)],
        input_output_aliases={len(operands) - 1: 0},
        scratch_shapes=[
            pltpu.VMEM((blocks * rows, lat), BF16),
            pltpu.VMEM((blocks, rows, lat), BF16),
            pltpu.SemaphoreType.DMA((2,)),
        ],
        compiler_params=params(16),
        name="second_step",
    )(*operands, sub_ids, *halo)[1]


def per_device(
    fine_latent,
    coarse_latent,
    adj_index,
    adj_weight,
    interp_slot,
    interp_weight,
    coarse_send,
    halo_sub_send,
    halo_dom_send,
    block_count,
    w_in,
    b_in,
    w_out,
    ln_gain,
):
    sub_ids = halo_sub_send[0].T
    dom_ids = halo_dom_send[0]
    adj_ids = adj_index.T
    payload = pick(coarse_latent, coarse_send.reshape(1, -1))
    received = lax.all_to_all(payload, ("dom", "sub"), split_axis=0, concat_axis=0, tiled=True)
    halo = second_hop(fine_latent, first_hop(fine_latent, sub_ids, payload), sub_ids, dom_ids)
    pool, other, interp, weights = first_step(
        received, interp_slot.T, interp_weight, fine_latent, halo, adj_ids, adj_weight, w_in, b_in,
        w_out, ln_gain, block_count, sub_ids,
    )
    halo = second_hop(pool, other, sub_ids, dom_ids)
    return second_step(
        pool, halo, weights, interp, adj_ids, w_in, b_in, w_out, ln_gain, block_count, sub_ids
    )


def solution(mesh):
    split = ("dom", "sub")
    placed = (
        P(split, None, None),
        P(split, None, None),
        P(split, None),
        P(split, None, None),
        P(split, None),
        P(split, None, None),
        P(split, None, None),
        P(split, None, None),
        P(split, None, None),
        P(split),
        P(),
        P(),
        P(),
        P(),
    )
    return jax.shard_map(
        per_device,
        mesh=mesh,
        in_specs=placed,
        out_specs=P(split, None, None),
        check_vma=False,
    )
```

```python
import functools

import jax
import jax.numpy as jnp
from jax import lax
from jax.experimental import pallas as pl
from jax.experimental.pallas import tpu as pltpu
from jax.sharding import PartitionSpec as P

BF16 = jnp.bfloat16
F32 = jnp.float32
SMEM = pl.BlockSpec(memory_space=pltpu.SMEM)
VMEM = pl.BlockSpec(memory_space=pltpu.VMEM)
ANY = pl.BlockSpec(memory_space=pl.ANY)
CORES = 2
WAYS = (1, 3, 2)


def in_hbm(array):
    return pltpu.with_memory_space_constraint(array, pltpu.HBM)


def in_vmem(array):
    return pltpu.with_memory_space_constraint(array, pltpu.VMEM)


def params(mib):
    return pltpu.CompilerParams(vmem_limit_bytes=mib << 20)


def blocks_like(count, latent):
    return jax.ShapeDtypeStruct((count,) + latent.shape[1:], BF16)


def chunked(source, target, sems):
    parts = sems.shape[0]
    size = source.shape[0] // parts
    return [
        pltpu.make_async_copy(
            source.at[pl.ds(part * size, size)], target.at[pl.ds(part * size, size)], sems.at[part]
        )
        for part in range(parts)
    ]


def start(copies):
    for copy in copies:
        copy.start()


def wait(copies):
    for copy in copies:
        copy.wait()


def copy_for_other_core(latent, sub_ids, out):
    slots, peers = sub_ids.shape
    me = lax.axis_index("sub")
    for way in range(peers // CORES):
        peer = me ^ (way * CORES + 1)
        for slot in range(slots):
            out[way * slots + slot] = latent[sub_ids[slot, peer]]


def copy_for_dom(latent, dom_ids, way, out):
    for slot in range(dom_ids.shape[1]):
        out[slot] = latent[dom_ids[way, slot]]


def copy_for_x(latent, sub_ids, passed, outs):
    slots = sub_ids.shape[0]
    me = lax.axis_index("sub")
    mine = (me % CORES) * slots
    for way, out in zip(WAYS, outs):
        for slot in range(slots):
            out[mine + slot] = latent[sub_ids[slot, me ^ (way * CORES)]]
            out[slots - mine + slot] = passed[way * slots + slot]


def first_hop_kernel(sub_ids, latent, after, other, sems):
    del after
    slots, peers = sub_ids.shape
    me = lax.axis_index("sub")
    copies = []
    for way in range(peers // CORES):
        peer = me ^ (way * CORES + 1)
        for slot in range(slots):
            place = way * slots + slot
            copies.append(
                pltpu.make_async_copy(
                    latent.at[sub_ids[slot, peer]], other.at[place], sems.at[place]
                )
            )
    start(copies)
    wait(copies)


def first_hop(latent, sub_ids, after):
    count = sub_ids.size // CORES
    return pl.pallas_call(
        first_hop_kernel,
        in_specs=[SMEM, ANY, ANY],
        out_specs=VMEM,
        out_shape=blocks_like(count, latent),
        scratch_shapes=[pltpu.SemaphoreType.DMA((count,))],
        compiler_params=params(8),
        name="first_hop",
    )(*map(in_hbm, (sub_ids, latent, after)))


def x_counts(sub_ids):
    slots, peers = sub_ids.shape
    return [slots * CORES] * (peers // CORES - 1)


def pick_kernel(ids, table, out, ids_held, held, staged, load_sems, sems):
    loads = [
        pltpu.make_async_copy(ids, ids_held, load_sems.at[0]),
        pltpu.make_async_copy(table, held, load_sems.at[1]),
    ]
    start(loads)
    wait(loads)
    copies = chunked(staged, out, sems)
    size = staged.shape[0] // len(copies)
    for part, copy in enumerate(copies):
        for slot in range(part * size, (part + 1) * size):
            staged[slot] = held[ids_held[0, slot]]
        copy.start()
    wait(copies)


def pick(coarse, ids):
    shape = (ids.shape[1],) + coarse.shape[1:]
    return pl.pallas_call(
        pick_kernel,
        in_specs=[ANY, ANY],
        out_specs=ANY,
        out_shape=pltpu.HBM(shape, BF16),
        scratch_shapes=[
            pltpu.SMEM(ids.shape, jnp.int32),
            pltpu.VMEM(coarse.shape, BF16),
            pltpu.VMEM(shape, BF16),
            pltpu.SemaphoreType.DMA((2,)),
            pltpu.SemaphoreType.DMA((8,)),
        ],
        compiler_params=params(8),
        name="pick",
    )(in_hbm(ids), in_hbm(coarse))


def repack_kernel(sub_ids, dom_ids, latent, passed, *outs):
    *pieces, up, down = outs
    copy_for_x(latent, sub_ids, passed, pieces)
    copy_for_dom(latent, dom_ids, 0, up)
    copy_for_dom(latent, dom_ids, 1, down)


def repack(latent, passed, sub_ids, dom_ids):
    counts = x_counts(sub_ids) + [dom_ids.shape[1]] * 2
    return pl.pallas_call(
        repack_kernel,
        in_specs=[SMEM, SMEM, VMEM, VMEM],
        out_specs=[VMEM] * len(counts),
        out_shape=[blocks_like(count, latent) for count in counts],
        compiler_params=params(8),
        name="repack",
    )(sub_ids, dom_ids, latent, passed)


def to_other_core(blocks):
    return lax.ppermute(blocks, "sub", [(i, i ^ 1) for i in range(lax.axis_size("sub"))])


def along_x(pieces):
    size = lax.axis_size("sub")
    return [
        lax.ppermute(piece, "sub", [(i, i ^ (way * CORES)) for i in range(size)])
        for way, piece in zip(WAYS, pieces)
    ]


def along_dom(blocks, distance):
    size = lax.axis_size("dom")
    return lax.ppermute(blocks, "dom", [(i, (i + distance) % size) for i in range(size)])


def second_hop(latent, other, sub_ids, dom_ids):
    passed = to_other_core(other)
    *pieces, up, down = repack(latent, passed, sub_ids, dom_ids)
    return [passed, *along_x(pieces), along_dom(up, 1), along_dom(down, -1)]


def fill_pool(pool, own, sub_ids, passed, pieces, below, above):
    slots, peers = sub_ids.shape
    me = lax.axis_index("sub")
    pool[pl.ds(own + (me ^ 1) * slots, slots)] = passed[:slots]
    for way, piece in zip(WAYS, pieces):
        first = own + (me // CORES ^ way) * CORES * slots
        pool[pl.ds(first, piece.shape[0])] = piece[...]
    end = own + peers * slots
    pool[pl.ds(end, below.shape[0])] = below[...]
    pool[pl.ds(end + below.shape[0], above.shape[0])] = above[...]
    clear_ends(pool, below.shape[0])


def copy_to_self(pool, sub_ids, own):
    slots = sub_ids.shape[0]
    me = lax.axis_index("sub")
    for slot in range(slots):
        pool[own + me * slots + slot] = pool[sub_ids[slot, me]]


def clear_ends(pool, count):
    end = pool.shape[0]
    zeros = jnp.zeros((count,) + pool.shape[1:], pool.dtype)

    @pl.when(lax.axis_index("dom") == 0)
    def _():
        pool[pl.ds(end - 2 * count, count)] = zeros

    @pl.when(lax.axis_index("dom") == lax.axis_size("dom") - 1)
    def _():
        pool[pl.ds(end - count, count)] = zeros


def tile_product(weights, table, ids, block, width):
    total = None
    rows = table.shape[1]
    for first in range(0, ids.shape[0], width):
        gathered = jnp.concatenate(
            [table[ids[first + tile, block]] for tile in range(width)], axis=0
        )
        part = jnp.dot(
            weights[block, :, first * rows : (first + width) * rows],
            gathered,
            preferred_element_type=F32,
        )
        total = part if total is None else total + part
    return total.astype(BF16)


def products(weights, table, ids, out, first, last):
    rows = table.shape[1]
    for block in range(first, last):
        out[pl.ds(block * rows, rows)] = tile_product(weights, table, ids, block, 4)


def node_network(hidden, latent, w_out, gain, live):
    hidden = jnp.maximum(hidden, 0.0).astype(BF16)
    out = jnp.dot(hidden, w_out, preferred_element_type=F32)
    average = jnp.mean(out, axis=-1, keepdims=True)
    centred = out - average
    variance = jnp.mean(centred * centred, axis=-1, keepdims=True)
    normed = centred * lax.rsqrt(variance + 1e-05) * gain
    updated = latent.astype(F32) + normed
    return jnp.where(live, updated, 0.0).astype(BF16)


def live_rows(count, first, size):
    return first + lax.broadcasted_iota(jnp.int32, (size, 1), 0) < count


def prepare_kernel(
    slots, received, weights, interp_weights, w_in, b_in, w_out, gain, latent,
    interp, held, pool, *rest,
):
    net, (slots_held, coarse, slots_sem, interp_sems, own_sem, in_sem, network_sems) = rest[:4], rest[4:]
    table = pltpu.make_async_copy(slots, slots_held, slots_sem)
    table.start()
    arriving = chunked(interp_weights, coarse, interp_sems)
    start(arriving)
    blocks = latent.shape[0]
    more = [
        pltpu.make_async_copy(latent, pool.at[pl.ds(0, blocks)], own_sem),
        pltpu.make_async_copy(weights, held, in_sem),
    ]
    more += [
        pltpu.make_async_copy(source, target, network_sems.at[position])
        for position, (source, target) in enumerate(zip((w_in, b_in, w_out, gain), net))
    ]
    table.wait()
    size = blocks // len(arriving)
    for part, copy in enumerate(arriving):
        copy.wait()
        if part == 0:
            start(more)
        products(coarse, received, slots_held, interp, part * size, (part + 1) * size)
    wait(more)


def prepare(received, slots, interp_weights, latent, pool, weights, network):
    blocks, rows, lat = latent.shape
    return pl.pallas_call(
        prepare_kernel,
        in_specs=[ANY, VMEM] + [ANY] * 7,
        out_specs=[VMEM] * 7,
        out_shape=[
            jax.ShapeDtypeStruct((blocks * rows, lat), BF16),
            pltpu.VMEM(weights.shape, BF16),
            pltpu.VMEM((pool, rows, lat), BF16),
            *(pltpu.VMEM(part.shape, part.dtype) for part in network),
        ],
        scratch_shapes=[
            pltpu.SMEM(slots.shape, jnp.int32),
            pltpu.VMEM(interp_weights.shape, BF16),
            pltpu.SemaphoreType.DMA,
            pltpu.SemaphoreType.DMA((2,)),
            pltpu.SemaphoreType.DMA,
            pltpu.SemaphoreType.DMA,
            pltpu.SemaphoreType.DMA((4,)),
        ],
        compiler_params=params(8),
        name="prepare",
    )(in_hbm(slots), received, *map(in_hbm, (weights, interp_weights, *network, latent)))


def first_kernel(
    count, ids, sub_ids, weights, interp, w_in, b_in, w_out, gain, pool_in, passed, *rest
):
    del pool_in
    ways = sub_ids.shape[1] // CORES - 1
    pieces, (below, above, pool, other, summed) = rest[:ways], rest[ways:]
    blocks = weights.shape[0]
    rows, lat = pool.shape[1:]
    fill_pool(pool, blocks, sub_ids, passed, pieces, below, above)
    copy_to_self(pool, sub_ids, blocks)
    products(weights, pool, ids, summed, 0, blocks)
    own = pool[pl.ds(0, blocks)].reshape(blocks * rows, lat)
    joined = jnp.concatenate([own, summed[...], interp[...]], axis=1)
    hidden = jnp.dot(joined, w_in[0], preferred_element_type=F32) + b_in[0:1]
    live = live_rows(count[0] * rows, 0, blocks * rows)
    new = node_network(hidden, own, w_out[0], gain[0:1], live)
    pool[pl.ds(0, blocks)] = new.reshape(blocks, rows, lat)
    copy_for_other_core(pool, sub_ids, other)
    copy_to_self(pool, sub_ids, blocks)


def first_step(pool, halo, weights, interp, ids, network, count, sub_ids):
    rows, lat = pool.shape[1:]
    blocks = weights.shape[0]
    operands = [count, ids, sub_ids, *map(in_vmem, (weights, interp, *network, pool))]
    return pl.pallas_call(
        first_kernel,
        in_specs=[SMEM] * 3 + [VMEM] * (7 + len(halo)),
        out_specs=[VMEM] * 2,
        out_shape=[
            pltpu.VMEM(pool.shape, BF16),
            jax.ShapeDtypeStruct((sub_ids.size // CORES, rows, lat), BF16),
        ],
        input_output_aliases={len(operands) - 1: 0},
        scratch_shapes=[pltpu.VMEM((blocks * rows, lat), BF16)],
        compiler_params=params(16),
        name="first_step",
    )(*operands, *halo)


def second_kernel(
    ids, count, weights, interp, w_in, b_in, w_out, gain, pool_in, sub_shape, passed, *rest
):
    del pool_in
    ways = sub_shape.shape[1] // CORES - 1
    last, below, above, *rest = rest
    pieces, rest = [*rest[: ways - 1], last], rest[ways - 1 :]
    pool, out, summed, staged, out_sems = rest
    blocks, rows, lat = staged.shape
    fill_pool(pool, blocks, sub_shape, passed, pieces, below, above)
    products(weights, pool, ids, summed, 0, blocks)
    copies = chunked(staged, out, out_sems)
    size = blocks // len(copies)
    for part, copy in enumerate(copies):
        mine = pl.ds(part * size, size)
        here = pl.ds(part * size * rows, size * rows)
        own = pool[mine].reshape(size * rows, lat)
        joined = jnp.concatenate([own, summed[here], interp[here]], axis=1)
        hidden = jnp.dot(joined, w_in[1], preferred_element_type=F32) + b_in[1:2]
        live = live_rows(count[0] * rows, part * size * rows, size * rows)
        new = node_network(hidden, own, w_out[1], gain[1:2], live)
        staged[mine] = new.reshape(size, rows, lat)
        copy.start()
    wait(copies)


def second_step(pool, halo, weights, interp, ids, network, count, sub_ids):
    rows, lat = pool.shape[1:]
    blocks = weights.shape[0]
    passed, *pieces, below, above = halo
    operands = [ids, count, *map(in_vmem, (weights, interp, *network, pool))]
    return pl.pallas_call(
        second_kernel,
        in_specs=[SMEM] * 2 + [VMEM] * 7 + [ANY] + [VMEM] * len(halo),
        out_specs=[VMEM, ANY],
        out_shape=[pltpu.VMEM(pool.shape, BF16), pltpu.HBM((blocks, rows, lat), BF16)],
        input_output_aliases={len(operands) - 1: 0},
        scratch_shapes=[
            pltpu.VMEM((blocks * rows, lat), BF16),
            pltpu.VMEM((blocks, rows, lat), BF16),
            pltpu.SemaphoreType.DMA((2,)),
        ],
        compiler_params=params(16),
        name="second_step",
    )(*operands, sub_ids, passed, *pieces[-1:], below, above, *pieces[:-1])[1]


def per_device(
    fine_latent,
    coarse_latent,
    adj_index,
    adj_weight,
    interp_slot,
    interp_weight,
    coarse_send,
    halo_sub_send,
    halo_dom_send,
    block_count,
    w_in,
    b_in,
    w_out,
    ln_gain,
):
    sub_ids = halo_sub_send[0].T
    dom_ids = halo_dom_send[0]
    adj_ids = adj_index.T
    payload = pick(coarse_latent, coarse_send.reshape(1, -1))
    received = lax.all_to_all(payload, ("dom", "sub"), split_axis=0, concat_axis=0, tiled=True)
    halo = second_hop(fine_latent, first_hop(fine_latent, sub_ids, payload), sub_ids, dom_ids)
    size = fine_latent.shape[0] + sub_ids.size + dom_ids.size
    interp, weights, pool, *network = prepare(
        received, interp_slot.T, interp_weight, fine_latent, size, adj_weight,
        (w_in, b_in, w_out, ln_gain),
    )
    pool, other = first_step(pool, halo, weights, interp, adj_ids, network, block_count, sub_ids)
    halo = second_hop(pool, other, sub_ids, dom_ids)
    return second_step(pool, halo, weights, interp, adj_ids, network, block_count, sub_ids)


def solution(mesh):
    split = ("dom", "sub")
    placed = (
        P(split, None, None),
        P(split, None, None),
        P(split, None),
        P(split, None, None),
        P(split, None),
        P(split, None, None),
        P(split, None, None),
        P(split, None, None),
        P(split, None, None),
        P(split),
        P(),
        P(),
        P(),
        P(),
    )
    return jax.shard_map(
        per_device,
        mesh=mesh,
        in_specs=placed,
        out_specs=P(split, None, None),
        check_vma=False,
    )
```
